256 devices in a mesh: dp: 2 (over core), expert: 16 (over x, y), etp: 8 (over z).
Axes of the slice: x: 4, y: 4, z: 8, core: 2. Of those that a mesh axis runs over, the one named last changes fastest.
Arguments:
- tokens_in: bfloat16 [4096, 4096], P(('dp', 'expert'), 'etp'), may hold values from -6 to 6
- grad_output: bfloat16 [4096, 4096], P(('dp', 'expert'), 'etp'), may hold values from -12 to 12
- routes: int32 [4096, 8], P(('dp', 'expert')), may hold values from 0 to 15, all different within a row; in each aligned block of 128 rows (0 to 127, 128 to 255, ...) at most 66 rows name the same one
- route_numer: int32 [4096, 8], P(('dp', 'expert')), may hold values from 1 to 16
- w_gate: bfloat16 [16, 1536, 4096], P('expert', None, 'etp'), may hold values from -0.09375 to 0.09375
- w_up: bfloat16 [16, 1536, 4096], P('expert', None, 'etp'), may hold values from -0.09375 to 0.09375
- w_down: bfloat16 [16, 1536, 4096], P('expert', None, 'etp'), may hold values from -0.15625 to 0.15625
Outputs:
- grad_input: bfloat16 [4096, 4096], P(('dp', 'expert'), 'etp')
- grad_w_gate: bfloat16 [16, 1536, 4096], P('expert', 'dp', 'etp')
- grad_w_up: bfloat16 [16, 1536, 4096], P('expert', 'dp', 'etp')
- grad_w_down: bfloat16 [16, 1536, 4096], P('expert', 'dp', 'etp')
The draws below stay inside these ranges and needn't reach their ends.
Inputs may be any that keep to these rules, and one draw needn't show every extreme that they name: `routes`: each row names 8 different experts. Within each aligned block of 128 rows (the rows of one index of dp and expert) no expert is named by more than 66 rows, and in every draw some expert is named by exactly 66 rows of some block.
All inputs are finite; a program needn't handle non-finite values.
Results may differ from the reference program's by a relative error of at most 0.03.
Values may be sent and summed in bfloat16 or wider, within the bound.
No kernel may reach another device: no remote copies, remote signals or barrier semaphores. Data moves between devices by JAX's collectives and lax.ppermute only.
A program may use at most 128 MiB of HBM per device.

```python
import math
import jax
import jax.numpy as jnp
import numpy as np
from jax import lax

D = 4096
FF = 1536
TOPK = 8
EXPERTS = 16
TOK_DEV = 128
CAP = 66
TOKENS = 4096
N_DP = 2
N_EXPERT = 16
N_ETP = 8


def set_ends(result, rng, low, largest):
    longest = result.shape.index(max(result.shape))
    spots = []
    for shift in (0, 1):
        where = [jax.random.randint(jax.random.fold_in(rng, axis), (), 0, length) for axis, length in enumerate(result.shape)]
        where[longest] = (where[longest] + shift) % result.shape[longest]
        spots.append(tuple(where))
    return result.at[spots[0]].set(low).at[spots[1]].set(largest)


def level_of(rng, extent, shards, low, top_value):
    def one(dim, parts):
        steps = jax.random.uniform(jax.random.fold_in(jax.random.fold_in(rng, 6), dim), (parts,), jnp.float32, low / len(shards), top_value / len(shards))
        return jnp.repeat(jnp.exp(steps), extent[dim] // parts).reshape((-1,) + (1,) * (len(extent) - dim - 1))

    level = one(*shards[0])
    for cut in shards[1:]:
        level = level * one(*cut)
    return level


def deal_out(stream_key, own, number, rows, number_of, top, most, slope):
    order = jax.random.permutation(stream_key, number_of)
    heavy_load, ordinary = portions_of(number_of, rows * top, most, slope, True), portions_of(number_of, rows * top, most, slope, False)
    places = jnp.arange(number_of)

    def named(lengths, offset_by):
        used = int((lengths > 0).sum())
        fixed = max(1, used // 4)
        shifted = fixed + (places - fixed + offset_by * (used - fixed)) % max(1, number_of - fixed)
        return jnp.zeros((number_of,), jnp.int32).at[order[jnp.where(places < fixed, places, shifted)]].set(jnp.asarray(lengths, jnp.int32))

    lengths = jnp.where(number % 4 == 0, named(heavy_load, number // 4), named(ordinary, number - number // 4 - 1))
    mixed = jax.random.permutation(jax.random.fold_in(own, 3), number_of)
    giver, receiver = mixed[0:number_of // 2 * 2:2], mixed[1:number_of // 2 * 2:2]
    room = jnp.minimum(lengths[giver] - 1, most - lengths[receiver]) // 2
    room = jnp.where((giver == order[0]) | (receiver == order[0]) | (lengths[receiver] == 0), 0, jnp.maximum(room, 0))
    shifted = jax.random.randint(jax.random.fold_in(own, 4), (number_of // 2,), 0, 1 << 20) % (room + 1)
    lengths = lengths.at[giver].add(-shifted).at[receiver].add(shifted)
    items = jnp.searchsorted(jnp.cumsum(lengths), jnp.arange(rows * top), side="right").astype(jnp.int32)
    grid = items.reshape(top, rows).T
    grid = grid[jax.random.permutation(jax.random.fold_in(own, 1), rows)]
    offset_by = jax.random.randint(jax.random.fold_in(own, 2), (rows, 1), 0, top)
    return jnp.take_along_axis(grid, (jnp.arange(top)[None, :] + offset_by) % top, axis=1)


def portions_of(number_of, total, most, slope, full):
    weights = [(1 << 20) // math.isqrt(grade ** slope) + 1 for grade in range(1, number_of + 1)]
    largest = most if full else min(most, max(-(-total // number_of), total * weights[0] // sum(weights)))
    least = 1 if total - largest >= number_of - 1 else 0
    given, rest = [largest] + [least] * (number_of - 1), total - largest - least * (number_of - 1)
    while rest > 0:
        movable = [i for i in range(1, number_of) if given[i] < largest] or [i for i in range(1, number_of) if given[i] < most]
        pool, remaining = sum([weights[i] for i in movable]), rest
        for i in movable:
            extra = min(most - given[i], max(1, remaining * weights[i] // pool), rest)
            given[i] = given[i] + extra
            rest = rest - extra
    return np.array(given)


def noise(stream_key, shape, deviation, limit, pieces=(), kind=jnp.bfloat16):
    result = jax.random.normal(stream_key, shape, jnp.float32) * deviation
    if len(pieces) > 0:
        result = level_of(stream_key, shape, pieces, -0.22, 0.18) * result
    return jnp.clip(result, min=-limit, max=limit).astype(kind)


def setup_inputs(seed: int = 0) -> dict:
    seeds = jax.random.split(jax.random.key(seed), 8)
    tokens_in = noise(seeds[0], (TOKENS, D), 1.0, 6.0, ((0, 32), (1, 8)))
    grad_output = noise(seeds[1], (TOKENS, D), 2.0, 12.0, ((0, 32), (1, 8)))
    routes_keys = jax.random.split(jax.random.fold_in(seeds[2], 1), TOKENS // TOK_DEV)
    routes_turns = jax.random.permutation(jax.random.fold_in(seeds[2], 3), TOKENS // TOK_DEV)
    routes = jax.vmap(lambda own, number: deal_out(jax.random.fold_in(seeds[2], 2), own, number, TOK_DEV, EXPERTS, TOPK, CAP, 2))(routes_keys, routes_turns).reshape((TOKENS, TOPK))
    route_numer = set_ends(jax.random.randint(seeds[3], (TOKENS, TOPK), 1, 17), jax.random.fold_in(seeds[3], 1), 1, 16).astype(jnp.int32)
    w_gate = noise(seeds[4], (EXPERTS, FF, D), D ** -0.5, 0.09375, ((0, 16), (2, 8)))
    w_up = noise(seeds[5], (EXPERTS, FF, D), D ** -0.5, 0.09375, ((0, 16), (2, 8)))
    w_down = noise(seeds[6], (EXPERTS, FF, D), FF ** -0.5, 0.15625, ((0, 16), (2, 8)))
    return {"tokens_in": tokens_in, "grad_output": grad_output, "routes": routes, "route_numer": route_numer, "w_gate": w_gate, "w_up": w_up, "w_down": w_down}


def rounded(value):
    return lax.optimization_barrier(value.astype(jnp.bfloat16)).astype(jnp.float32)


def slot_layout(route_blocks, shares, expert):
    matches = route_blocks == expert
    member = jnp.sum(matches.astype(jnp.int32), axis=2)
    weight = jnp.sum(jnp.where(matches, shares, jnp.zeros_like(shares)), axis=2)
    position = jnp.cumsum(member, axis=1) - member
    slot_ids = jnp.arange(CAP, dtype=jnp.int32)
    placer = member[:, None, :] * (position[:, None, :] == slot_ids[None, :, None]).astype(jnp.int32)
    token_ids = jnp.arange(TOK_DEV, dtype=jnp.int32)
    source = jnp.sum(placer * token_ids[None, None, :], axis=2).astype(jnp.int32)
    filled = jnp.sum(placer, axis=2)
    slot_weight = jnp.sum(placer.astype(jnp.float32) * weight[:, None, :], axis=2)
    return source, filled, slot_weight


def slice_sums(rows, weight, feature_slice):
    total = jnp.zeros((rows.shape[0], weight.shape[0]), jnp.float32)
    for column in range(N_ETP):
        first = column * feature_slice
        last = first + feature_slice
        total = total + rounded(jnp.dot(rows[:, first:last], weight[:, first:last].T, preferred_element_type=jnp.float32))
    return total


def reference(tokens_in, grad_output, routes, route_numer, w_gate, w_up, w_down):
    blocks = N_DP * N_EXPERT
    width = tokens_in.shape[1]
    token_blocks = tokens_in.reshape(blocks, TOK_DEV, width)
    grad_blocks = grad_output.reshape(blocks, TOK_DEV, width)
    route_blocks = routes.reshape(blocks, TOK_DEV, TOPK)
    numerators = route_numer.astype(jnp.float32)
    shares = (numerators / jnp.sum(numerators, axis=1, keepdims=True)).reshape(blocks, TOK_DEV, TOPK)
    feature_slice = width // N_ETP
    group_rows = N_EXPERT * CAP
    pick = jax.vmap(lambda table, index: table[index])
    spread = jax.vmap(lambda values, index: jax.ops.segment_sum(values, index, num_segments=TOK_DEV))

    def per_expert(totals, expert):
        source, filled, slot_weight = slot_layout(route_blocks, shares, expert)
        row_slots = pick(token_blocks, source) * filled[:, :, None].astype(jnp.bfloat16)
        grad_sel = pick(grad_blocks, source).astype(jnp.float32)
        grad_slots = (slot_weight[:, :, None] * grad_sel).astype(jnp.bfloat16)
        rows_flat = row_slots.reshape(blocks * CAP, width)
        grads_flat = grad_slots.reshape(blocks * CAP, width)
        gate_w = w_gate[expert]
        up_w = w_up[expert]
        down_w = w_down[expert]
        gate_pre = slice_sums(rows_flat, gate_w, feature_slice)
        up_pre = slice_sums(rows_flat, up_w, feature_slice)
        grad_hidden = slice_sums(grads_flat, down_w, feature_slice)
        sigmoid_gate = jax.nn.sigmoid(gate_pre)
        activated = gate_pre * sigmoid_gate
        hidden = (activated * up_pre).astype(jnp.bfloat16)
        grad_gate = (grad_hidden * up_pre * sigmoid_gate * (1.0 + gate_pre * (1.0 - sigmoid_gate))).astype(jnp.bfloat16)
        grad_up = (grad_hidden * activated).astype(jnp.bfloat16)
        sums_gate = jnp.zeros((FF, width), jnp.float32)
        sums_up = jnp.zeros((FF, width), jnp.float32)
        sums_down = jnp.zeros((FF, width), jnp.float32)
        for group in range(N_DP):
            first = group * group_rows
            last = first + group_rows
            sums_gate = sums_gate + rounded(jnp.dot(grad_gate[first:last].T, rows_flat[first:last], preferred_element_type=jnp.float32))
            sums_up = sums_up + rounded(jnp.dot(grad_up[first:last].T, rows_flat[first:last], preferred_element_type=jnp.float32))
            sums_down = sums_down + rounded(jnp.dot(hidden[first:last].T, grads_flat[first:last], preferred_element_type=jnp.float32))
        slot_grad = jnp.dot(grad_gate, gate_w, preferred_element_type=jnp.float32)
        slot_grad = rounded(slot_grad + jnp.dot(grad_up, up_w, preferred_element_type=jnp.float32))
        slot_total = slot_grad.reshape(blocks, CAP, width) * filled[:, :, None].astype(jnp.float32)
        totals = totals + spread(slot_total, source)
        return totals, (sums_gate.astype(jnp.bfloat16), sums_up.astype(jnp.bfloat16), sums_down.astype(jnp.bfloat16))

    start = jnp.zeros((blocks, TOK_DEV, width), jnp.float32)
    totals, stacks = lax.scan(per_expert, start, jnp.arange(EXPERTS, dtype=jnp.int32))
    grad_input = totals.reshape(blocks * TOK_DEV, width).astype(jnp.bfloat16)
    return grad_input, stacks[0], stacks[1], stacks[2]
```

```python
import functools
import jax
import jax.numpy as jnp
from jax import lax
from jax.experimental import pallas as pl
from jax.experimental.pallas import tpu as pltpu
from jax.sharding import PartitionSpec as P

EXPERTS = 16
CAP = 66
PAD = 72
TOK = 128
RING = 8
ROWS = EXPERTS * CAP
HALF = ROWS // 2
WID = 512
FF = 1536
PART = FF // (2 * RING)
CH = 2 * PART
PACK = 2 * CH
TILE = 176
STEPS = HALF // TILE
F32 = jnp.float32
BF = jnp.bfloat16
NT = (((1,), (1,)), ((), ()))
NN = (((1,), (0,)), ((), ()))
TN = (((0,), (0,)), ((), ()))


def params(mib=24):
    return pltpu.CompilerParams(
        dimension_semantics=("arbitrary",), vmem_limit_bytes=mib * 1024 * 1024
    )


def cost(flops, nbytes):
    return pl.CostEstimate(flops=flops, bytes_accessed=nbytes, transcendentals=0)


def one_hot(first, count, rt):
    ids = lax.broadcasted_iota(jnp.int32, (count, 8, TOK), 0) + first
    match = jnp.where(rt[None] == ids, 1.0, 0.0)
    member = jnp.sum(match, axis=1)
    below = lax.broadcasted_iota(jnp.int32, (TOK, TOK), 0) < lax.broadcasted_iota(
        jnp.int32, (TOK, TOK), 1
    )
    before = lax.dot_general(
        member.astype(BF), jnp.where(below, 1.0, 0.0).astype(BF), NN, preferred_element_type=F32
    )
    place = jnp.where(member > 0.0, before, -1.0)
    slot = lax.broadcasted_iota(jnp.int32, (count, PAD, TOK), 1).astype(F32)
    return jnp.where(place[:, None, :] == slot, 1.0, 0.0), match


def slots_kernel(rt_ref, nt_ref, x_ref, g_ref, xs_ref, gs_ref):
    count = xs_ref.shape[0]
    pick, match = one_hot(pl.program_id(0) * count, count, rt_ref[...])
    num = nt_ref[...].astype(F32)
    share = num / jnp.sum(num, axis=0, keepdims=True)
    weight = jnp.sum(match * share[None], axis=1)
    slot_weight = jnp.sum(pick * weight[:, None, :], axis=2, keepdims=True)
    flat = pick.reshape(count * PAD, TOK).astype(BF)
    xs = lax.dot_general(flat, x_ref[...], NN, preferred_element_type=F32)
    gs = lax.dot_general(flat, g_ref[...], NN, preferred_element_type=F32)
    xs_ref[...] = xs.reshape(count, PAD, WID)[:, :CAP].astype(BF)
    gs_ref[...] = (gs.reshape(count, PAD, WID) * slot_weight)[:, :CAP].astype(BF)


def build_slots(rt, nt, x, g):
    count = 4
    whole = lambda shape: pl.BlockSpec(shape, lambda i: (0,) * len(shape))
    out = pl.BlockSpec((count, CAP, WID), lambda i: (i, 0, 0))
    return pl.pallas_call(
        slots_kernel,
        grid=(EXPERTS // count,),
        in_specs=[whole((8, TOK)), whole((8, TOK)), whole((TOK, WID)), whole((TOK, WID))],
        out_specs=[out, out],
        out_shape=[jax.ShapeDtypeStruct((EXPERTS, CAP, WID), BF)] * 2,
        compiler_params=params(),
        name="build_slots",
    )(rt, nt, x, g)


def back_kernel(rt_ref, v_ref, o_ref, acc, wide):
    count = v_ref.shape[0]
    pick, _ = one_hot(pl.program_id(0) * count, count, rt_ref[...])
    wide[...] = jnp.zeros_like(wide)
    wide[:, :CAP, :] = v_ref[...].astype(F32)
    part = lax.dot_general(
        pick.reshape(count * PAD, TOK).astype(BF),
        wide[...].reshape(count * PAD, WID).astype(BF),
        TN,
        preferred_element_type=F32,
    )

    @pl.when(pl.program_id(0) == 0)
    def _():
        acc[...] = part

    @pl.when(pl.program_id(0) > 0)
    def _():
        acc[...] += part

    @pl.when(pl.program_id(0) == pl.num_programs(0) - 1)
    def _():
        o_ref[...] = acc[...].astype(BF)


def gather_back(rt, values):
    count = 4
    return pl.pallas_call(
        back_kernel,
        grid=(EXPERTS // count,),
        in_specs=[
            pl.BlockSpec((8, TOK), lambda i: (0, 0)),
            pl.BlockSpec((count, CAP, WID), lambda i: (i, 0, 0)),
        ],
        out_specs=pl.BlockSpec((TOK, WID), lambda i: (0, 0)),
        out_shape=jax.ShapeDtypeStruct((TOK, WID), BF),
        scratch_shapes=[pltpu.VMEM((TOK, WID), F32), pltpu.VMEM((count, PAD, WID), F32)],
        compiler_params=params(),
        name="gather_back",
    )(rt, values)


def padded(w_ref):
    w = w_ref[...].reshape(CH, WID)
    zero = jnp.zeros((64, WID), BF)
    return jnp.concatenate([w, zero], axis=0), jnp.concatenate([zero, w], axis=0)


def partial_sums(rows_ref, w_ref, recv_ref):
    low, high = padded(w_ref)
    d1 = lax.dot_general(rows_ref[0], low, NT, preferred_element_type=F32)
    d2 = lax.dot_general(rows_ref[1], high, NT, preferred_element_type=F32)
    blocks = [d1[:, :128], d1[:, 128:] + d2[:, :128], d2[:, 128:]]
    if recv_ref is not None:
        blocks = [b + recv_ref[:, 128 * i : 128 * (i + 1)].astype(F32) for i, b in enumerate(blocks)]
    return blocks


def rs_kernel(first, own_ref, rows_ref, w_ref, *rest):
    recv_ref, o_ref = (None, rest[0]) if first else rest
    for i, b in enumerate(partial_sums(rows_ref, w_ref, recv_ref)):
        o_ref[:, 128 * i : 128 * (i + 1)] = b.astype(BF)


ROW_SPEC = pl.BlockSpec((2, TILE, WID), lambda i, own: (0, i, 0))
PACK_SPEC = pl.BlockSpec((TILE, PACK), lambda i, own: (i, 0))
PACK_BF = jax.ShapeDtypeStruct((HALF, PACK), BF)
PACK_F32 = jax.ShapeDtypeStruct((HALF, PACK), F32)


def w_spec(t):
    return pl.BlockSpec((2, PART, WID), lambda i, own: (0, own[t], 0))


def call(kernel, name, in_specs, out_specs, out_shape, flops, nbytes, scratch=(), aliases=None):
    return pl.pallas_call(
        kernel,
        grid_spec=pltpu.PrefetchScalarGridSpec(
            num_scalar_prefetch=1,
            grid=(STEPS,),
            in_specs=in_specs,
            out_specs=out_specs,
            scratch_shapes=scratch,
        ),
        out_shape=out_shape,
        input_output_aliases=aliases or {},
        compiler_params=params(),
        cost_estimate=cost(flops, nbytes),
        name=name,
    )


PROD = 2 * ROWS * CH * WID


def rs_step(t, own, rows, w, recv):
    first = recv is None
    return call(
        functools.partial(rs_kernel, first),
        "rs_step",
        [ROW_SPEC, w_spec(t)] + ([] if first else [PACK_SPEC]),
        PACK_SPEC,
        PACK_BF,
        PROD,
        2_500_000,
    )(own, rows, w, *(() if first else (recv,)))


def hidden_kernel(own_ref, rows_ref, wg_ref, wu_ref, rg_ref, ru_ref, gp_ref, up_ref, h_ref):
    gate = partial_sums(rows_ref, wg_ref, rg_ref)
    up = partial_sums(rows_ref, wu_ref, ru_ref)
    for i in range(3):
        lanes = slice(128 * i, 128 * (i + 1))
        gp_ref[:, lanes] = gate[i]
        up_ref[:, lanes] = up[i]
        h_ref[:, lanes] = (gate[i] * jax.nn.sigmoid(gate[i]) * up[i]).astype(BF)


def hidden_step(own, rows, wg, wu, rg, ru):
    return call(
        hidden_kernel,
        "hidden_step",
        [ROW_SPEC, w_spec(0), w_spec(0), PACK_SPEC, PACK_SPEC],
        [PACK_SPEC] * 3,
        [PACK_F32, PACK_F32, PACK_BF],
        2 * PROD,
        5_000_000,
    )(own, rows, wg, wu, rg, ru)


def grads_kernel(own_ref, rows_ref, w_ref, r_ref, gp_ref, up_ref, gg_ref, gu_ref):
    grad = partial_sums(rows_ref, w_ref, r_ref)
    for i in range(3):
        lanes = slice(128 * i, 128 * (i + 1))
        gate, up = gp_ref[:, lanes], up_ref[:, lanes]
        sig = jax.nn.sigmoid(gate)
        gg_ref[:, lanes] = (grad[i] * up * sig * (1.0 + gate * (1.0 - sig))).astype(BF)
        gu_ref[:, lanes] = (grad[i] * (gate * sig)).astype(BF)


def grads_step(own, rows, w, recv, gate, up):
    return call(
        grads_kernel,
        "grads_step",
        [ROW_SPEC, w_spec(0), PACK_SPEC, PACK_SPEC, PACK_SPEC],
        [PACK_SPEC] * 2,
        [PACK_BF] * 2,
        PROD,
        5_000_000,
    )(own, rows, w, recv, gate, up)


def weight_grad(piece, rows_ref):
    a = lax.dot_general(piece[:, : CH + 64], rows_ref[0], TN, preferred_element_type=F32)
    b = lax.dot_general(piece[:, CH - 64 :], rows_ref[1], TN, preferred_element_type=F32)
    return a[:CH] + b[64:]


def split_store(own_ref, total, keep_ref, send_ref, k):
    mine = own_ref[RING] == 0
    low, high = total[:PART].astype(BF), total[PART:].astype(BF)
    keep_ref[k] = jnp.where(mine, low, high)
    send_ref[k] = jnp.where(mine, high, low)


def accumulate(acc, k, part):
    @pl.when(pl.program_id(0) == 0)
    def _():
        acc[k] = part

    @pl.when(pl.program_id(0) > 0)
    def _():
        acc[k] += part


def ag_kernel(first, last, own_ref, pg_ref, pu_ref, rows_ref, wg_ref, wu_ref, *rest):
    sg_ref = None if first else rest[0]
    keep_ref, send_ref, out_ref, acc = rest[-4:]
    sums = [0.0, 0.0] if first else [sg_ref[0], sg_ref[1]]
    for k, (p_ref, w_ref) in enumerate(((pg_ref, wg_ref), (pu_ref, wu_ref))):
        piece = p_ref[...]
        low, high = padded(w_ref)
        sums[0] += lax.dot_general(piece[:, : CH + 64], low, NN, preferred_element_type=F32)
        sums[1] += lax.dot_general(piece[:, CH - 64 :], high, NN, preferred_element_type=F32)
        accumulate(acc, k, weight_grad(piece, rows_ref))
    for h in range(2):
        out_ref[h] = sums[h].astype(out_ref.dtype)

    @pl.when(pl.program_id(0) == STEPS - 1)
    def _():
        for k in range(2):
            split_store(own_ref, acc[k], keep_ref, send_ref, k)


def grad_spec(kinds):
    return pl.BlockSpec((kinds, PART, WID), lambda i, own: (0, 0, 0))


def ag_step(t, own, pg, pu, rows, wg, wu, sg):
    first, last = sg is None, t == RING - 1
    kept = jax.ShapeDtypeStruct((2, PART, WID), BF)
    return call(
        functools.partial(ag_kernel, first, last),
        "ag_step",
        [PACK_SPEC, PACK_SPEC, ROW_SPEC, w_spec(t), w_spec(t)] + ([] if first else [ROW_SPEC]),
        [grad_spec(2), grad_spec(2), ROW_SPEC],
        [kept, kept, jax.ShapeDtypeStruct((2, HALF, WID), BF if last else F32)],
        4 * PROD,
        7_000_000,
        [pltpu.VMEM((2, CH, WID), F32)],
        {6: 2} if not first and not last else None,
    )(own, pg, pu, rows, wg, wu, *(() if first else (sg,)))


def down_kernel(own_ref, ph_ref, rows_ref, keep_ref, send_ref, acc):
    accumulate(acc, 0, weight_grad(ph_ref[...], rows_ref))

    @pl.when(pl.program_id(0) == STEPS - 1)
    def _():
        split_store(own_ref, acc[0], keep_ref, send_ref, 0)


def down_step(t, own, ph, rows):
    kept = jax.ShapeDtypeStruct((1, PART, WID), BF)
    return call(
        down_kernel,
        "down_step",
        [PACK_SPEC, ROW_SPEC],
        [grad_spec(1), grad_spec(1)],
        [kept, kept],
        PROD,
        2_000_000,
        [pltpu.VMEM((1, CH, WID), F32)],
    )(own, ph, rows)


def merge_kernel(kinds, own_ref, *refs):
    keeps, recvs, outs = refs[:RING], refs[RING : 2 * RING], refs[2 * RING :]
    for t in range(RING):
        place = pl.ds(pl.multiple_of(own_ref[t] * PART, PART), PART)
        for k in range(kinds):
            total = keeps[t][k].astype(F32) + recvs[(RING - t) % RING][k].astype(F32)
            outs[k][place, :] = total.astype(BF)


def merge(own, keeps, recvs):
    kinds = keeps[0].shape[0]
    return pl.pallas_call(
        functools.partial(merge_kernel, kinds),
        grid_spec=pltpu.PrefetchScalarGridSpec(
            num_scalar_prefetch=1,
            grid=(1,),
            in_specs=[grad_spec(kinds)] * (2 * RING),
            out_specs=[pl.BlockSpec((FF // 2, WID), lambda i, own: (0, 0))] * kinds,
        ),
        out_shape=[jax.ShapeDtypeStruct((FF // 2, WID), BF)] * kinds,
        compiler_params=params(),
        name="merge",
    )(own, *keeps, *recvs)


def ring_hop(x):
    up = [(i, (i + 1) % RING) for i in range(RING)]
    down = [(RING + i, RING + (i - 1) % RING) for i in range(RING)]
    return lax.ppermute(x, ("dp", "etp"), up + down)


def swap(x):
    return lax.ppermute(x, "dp", [(0, 1), (1, 0)])


def exchange(x):
    return lax.all_to_all(x, "expert", split_axis=0, concat_axis=0, tiled=True)


def per_device(tokens_in, grad_output, routes, route_numer, w_gate, w_up, w_down):
    dp, z = lax.axis_index("dp"), lax.axis_index("etp")
    sign = 1 - 2 * dp
    hops = jnp.arange(RING, dtype=jnp.int32)
    own = jnp.concatenate([(z - sign * hops) % RING, dp[None]]).astype(jnp.int32)
    wg, wu, wd = (w.reshape(2, FF // 2, WID) for w in (w_gate, w_up, w_down))
    rt, nt = routes.T, route_numer.T

    x_send, g_send = build_slots(rt, nt, tokens_in, grad_output)
    xs = exchange(x_send).reshape(2, HALF, WID)
    gs = exchange(g_send).reshape(2, HALF, WID)

    gate, up = rs_step(1, own, xs, wg, None), rs_step(1, own, xs, wu, None)
    for t in range(2, RING):
        gate, up = ring_hop(gate), ring_hop(up)
        gate, up = rs_step(t, own, xs, wg, gate), rs_step(t, own, xs, wu, up)
    gate, up = ring_hop(gate), ring_hop(up)
    gate_pre, up_pre, hidden = hidden_step(own, xs, wg, wu, gate, up)

    back = rs_step(1, own, gs, wd, None)
    hid_keep, hid_recv = [], []

    def down(t, piece):
        keep, send = down_step(t, own, piece, gs)
        hid_keep.append(keep)
        hid_recv.append(swap(send))

    down(0, hidden)
    for t in range(2, RING + 1):
        back, hidden = ring_hop(back), ring_hop(hidden)
        if t < RING:
            back = rs_step(t, own, gs, wd, back)
        down(t - 1, hidden)
    pg, pu = grads_step(own, gs, wd, back, gate_pre, up_pre)

    keeps, recvs, sg = [], [], None
    for t in range(RING):
        if t > 0:
            pg, pu = ring_hop(pg), ring_hop(pu)
        keep, send, sg = ag_step(t, own, pg, pu, xs, wg, wu, sg)
        keeps.append(keep)
        recvs.append(swap(send))
    returned = exchange(sg.reshape(EXPERTS, CAP, WID))
    grad_input = gather_back(rt, returned)
    (grad_down,) = merge(own, hid_keep, hid_recv)
    grad_gate, grad_up = merge(own, keeps, recvs)
    return (grad_input, grad_gate[None], grad_up[None], grad_down[None])


def solution(mesh):
    placed = (
        P(("dp", "expert"), "etp"),
        P(("dp", "expert"), "etp"),
        P(("dp", "expert"), None),
        P(("dp", "expert"), None),
        P("expert", None, "etp"),
        P("expert", None, "etp"),
        P("expert", None, "etp"),
    )
    return jax.shard_map(
        per_device,
        mesh=mesh,
        in_specs=placed,
        out_specs=(
            P(("dp", "expert"), "etp"),
            P("expert", "dp", "etp"),
            P("expert", "dp", "etp"),
            P("expert", "dp", "etp"),
        ),
        check_vma=False,
    )
```

```python
import functools
import jax
import jax.numpy as jnp
from jax import lax
from jax.experimental import pallas as pl
from jax.experimental.pallas import tpu as pltpu
from jax.sharding import PartitionSpec as P

EXPERTS = 16
CAP = 66
PAD = 72
TOK = 128
RING = 8
ROWS = EXPERTS * CAP
HALF = ROWS // 2
WID = 512
FF = 1536
PART = FF // (2 * RING)
CH = 2 * PART
PACK = 2 * CH
TILE = 176
STEPS = HALF // TILE
F32 = jnp.float32
BF = jnp.bfloat16
NT = (((1,), (1,)), ((), ()))
NN = (((1,), (0,)), ((), ()))
TN = (((0,), (0,)), ((), ()))


def params(mib=12):
    return pltpu.CompilerParams(
        dimension_semantics=("arbitrary",), vmem_limit_bytes=mib * 1024 * 1024
    )


def cost(flops, nbytes):
    return pl.CostEstimate(flops=flops, bytes_accessed=nbytes, transcendentals=0)


def one_hot(first, count, rt):
    ids = lax.broadcasted_iota(jnp.int32, (count, 8, TOK), 0) + first
    match = jnp.where(rt[None] == ids, 1.0, 0.0)
    member = jnp.sum(match, axis=1)
    below = lax.broadcasted_iota(jnp.int32, (TOK, TOK), 0) < lax.broadcasted_iota(
        jnp.int32, (TOK, TOK), 1
    )
    before = lax.dot_general(
        member.astype(BF), jnp.where(below, 1.0, 0.0).astype(BF), NN, preferred_element_type=F32
    )
    place = jnp.where(member > 0.0, before, -1.0)
    slot = lax.broadcasted_iota(jnp.int32, (count, PAD, TOK), 1).astype(F32)
    return jnp.where(place[:, None, :] == slot, 1.0, 0.0), match


def slots_kernel(rt_ref, nt_ref, v_ref, o_ref):
    count = o_ref.shape[0]
    pick, match = one_hot(pl.program_id(0) * count, count, rt_ref[...])
    flat = pick.reshape(count * PAD, TOK).astype(BF)
    rows = lax.dot_general(flat, v_ref[...], NN, preferred_element_type=F32)
    rows = rows.reshape(count, PAD, WID)
    if nt_ref is not None:
        num = nt_ref[...].astype(F32)
        share = num / jnp.sum(num, axis=0, keepdims=True)
        weight = jnp.sum(match * share[None], axis=1)
        rows = rows * jnp.sum(pick * weight[:, None, :], axis=2, keepdims=True)
    o_ref[...] = rows[:, :CAP].astype(BF)


def plain_slots_kernel(rt_ref, v_ref, o_ref):
    slots_kernel(rt_ref, None, v_ref, o_ref)


def build_slots(rt, nt, values):
    count = 4
    whole = lambda x: pl.BlockSpec(x.shape, lambda i: (0, 0))
    args = [rt, values] if nt is None else [rt, nt, values]
    return pl.pallas_call(
        plain_slots_kernel if nt is None else slots_kernel,
        grid=(EXPERTS // count,),
        in_specs=[whole(x) for x in args],
        out_specs=pl.BlockSpec((count, CAP, WID), lambda i: (i, 0, 0)),
        out_shape=jax.ShapeDtypeStruct((EXPERTS, CAP, WID), BF),
        compiler_params=params(56),
        cost_estimate=cost(2 * EXPERTS * PAD * TOK * WID, 1_500_000),
        name="build_slots",
    )(*args)


def back_kernel(rt_ref, v_ref, o_ref, acc, wide):
    count = v_ref.shape[0]
    pick, _ = one_hot(pl.program_id(0) * count, count, rt_ref[...])
    wide[...] = jnp.zeros_like(wide)
    wide[:, :CAP, :] = v_ref[...].astype(F32)
    part = lax.dot_general(
        pick.reshape(count * PAD, TOK).astype(BF),
        wide[...].reshape(count * PAD, WID).astype(BF),
        TN,
        preferred_element_type=F32,
    )

    @pl.when(pl.program_id(0) == 0)
    def _():
        acc[...] = part

    @pl.when(pl.program_id(0) > 0)
    def _():
        acc[...] += part

    @pl.when(pl.program_id(0) == pl.num_programs(0) - 1)
    def _():
        o_ref[...] = acc[...].astype(BF)


def gather_back(rt, values):
    count = 4
    return pl.pallas_call(
        back_kernel,
        grid=(EXPERTS // count,),
        in_specs=[
            pl.BlockSpec((8, TOK), lambda i: (0, 0)),
            pl.BlockSpec((count, CAP, WID), lambda i: (i, 0, 0)),
        ],
        out_specs=pl.BlockSpec((TOK, WID), lambda i: (0, 0)),
        out_shape=jax.ShapeDtypeStruct((TOK, WID), BF),
        scratch_shapes=[pltpu.VMEM((TOK, WID), F32), pltpu.VMEM((count, PAD, WID), F32)],
        compiler_params=params(),
        name="gather_back",
    )(rt, values)


def padded(w_ref):
    w = w_ref[...].reshape(CH, WID)
    zero = jnp.zeros((64, WID), BF)
    return jnp.concatenate([w, zero], axis=0), jnp.concatenate([zero, w], axis=0)


def partial_sums(rows_ref, w_ref, recv_ref):
    low, high = padded(w_ref)
    d1 = lax.dot_general(rows_ref[0], low, NT, preferred_element_type=F32)
    d2 = lax.dot_general(rows_ref[1], high, NT, preferred_element_type=F32)
    blocks = [d1[:, :128], d1[:, 128:] + d2[:, :128], d2[:, 128:]]
    if recv_ref is not None:
        blocks = [b + recv_ref[:, 128 * i : 128 * (i + 1)].astype(F32) for i, b in enumerate(blocks)]
    return blocks


def rs_kernel(first, own_ref, rows_ref, w_ref, *rest):
    recv_ref, o_ref = (None, rest[0]) if first else rest
    for i, b in enumerate(partial_sums(rows_ref, w_ref, recv_ref)):
        o_ref[:, 128 * i : 128 * (i + 1)] = b.astype(BF)


ROW_SPEC = pl.BlockSpec((2, TILE, WID), lambda i, own: (0, i, 0))
PACK_SPEC = pl.BlockSpec((TILE, PACK), lambda i, own: (i, 0))
PACK_BF = jax.ShapeDtypeStruct((HALF, PACK), BF)
PACK_F32 = jax.ShapeDtypeStruct((HALF, PACK), F32)


def w_spec(t):
    return pl.BlockSpec((2, PART, WID), lambda i, own: (0, own[t], 0))


def call(kernel, name, in_specs, out_specs, out_shape, flops, nbytes, scratch=(), aliases=None):
    return pl.pallas_call(
        kernel,
        grid_spec=pltpu.PrefetchScalarGridSpec(
            num_scalar_prefetch=1,
            grid=(STEPS,),
            in_specs=in_specs,
            out_specs=out_specs,
            scratch_shapes=scratch,
        ),
        out_shape=out_shape,
        input_output_aliases=aliases or {},
        compiler_params=params(),
        cost_estimate=cost(flops, nbytes),
        name=name,
    )


PROD = 2 * ROWS * CH * WID


def rs_step(t, own, rows, w, recv):
    first = recv is None
    return call(
        functools.partial(rs_kernel, first),
        "rs_step",
        [ROW_SPEC, w_spec(t)] + ([] if first else [PACK_SPEC]),
        PACK_SPEC,
        PACK_BF,
        PROD,
        2_500_000,
    )(own, rows, w, *(() if first else (recv,)))


def hidden_kernel(own_ref, rows_ref, wg_ref, wu_ref, rg_ref, ru_ref, gp_ref, up_ref, h_ref):
    gate = partial_sums(rows_ref, wg_ref, rg_ref)
    up = partial_sums(rows_ref, wu_ref, ru_ref)
    for i in range(3):
        lanes = slice(128 * i, 128 * (i + 1))
        gp_ref[:, lanes] = gate[i]
        up_ref[:, lanes] = up[i]
        h_ref[:, lanes] = (gate[i] * jax.nn.sigmoid(gate[i]) * up[i]).astype(BF)


def hidden_step(own, rows, wg, wu, rg, ru):
    return call(
        hidden_kernel,
        "hidden_step",
        [ROW_SPEC, w_spec(0), w_spec(0), PACK_SPEC, PACK_SPEC],
        [PACK_SPEC] * 3,
        [PACK_F32, PACK_F32, PACK_BF],
        2 * PROD,
        5_000_000,
    )(own, rows, wg, wu, rg, ru)


def grads_kernel(own_ref, rows_ref, w_ref, r_ref, gp_ref, up_ref, gg_ref, gu_ref):
    grad = partial_sums(rows_ref, w_ref, r_ref)
    for i in range(3):
        lanes = slice(128 * i, 128 * (i + 1))
        gate, up = gp_ref[:, lanes], up_ref[:, lanes]
        sig = jax.nn.sigmoid(gate)
        gg_ref[:, lanes] = (grad[i] * up * sig * (1.0 + gate * (1.0 - sig))).astype(BF)
        gu_ref[:, lanes] = (grad[i] * (gate * sig)).astype(BF)


def grads_step(own, rows, w, recv, gate, up):
    return call(
        grads_kernel,
        "grads_step",
        [ROW_SPEC, w_spec(0), PACK_SPEC, PACK_SPEC, PACK_SPEC],
        [PACK_SPEC] * 2,
        [PACK_BF] * 2,
        PROD,
        5_000_000,
    )(own, rows, w, recv, gate, up)


def weight_grad(piece, rows_ref):
    a = lax.dot_general(piece[:, : CH + 64], rows_ref[0], TN, preferred_element_type=F32)
    b = lax.dot_general(piece[:, CH - 64 :], rows_ref[1], TN, preferred_element_type=F32)
    return a[:CH] + b[64:]


def grad_chunk(own_ref, piece, rows_ref, acc, keep_ref, send_ref):
    part = weight_grad(piece, rows_ref)

    @pl.when(pl.program_id(0) == 0)
    def _():
        acc[...] = part

    @pl.when(pl.program_id(0) > 0)
    def _():
        acc[...] += part

    @pl.when(pl.program_id(0) == STEPS - 1)
    def _():
        mine = own_ref[RING] == 0
        low, high = acc[:PART].astype(BF), acc[PART:].astype(BF)
        keep_ref[0] = jnp.where(mine, low, high)
        send_ref[0] = jnp.where(mine, high, low)


def slot_sums(p_ref, w_ref, sums):
    low, high = padded(w_ref)
    return [
        sums[0] + lax.dot_general(p_ref[:, : CH + 64], low, NN, preferred_element_type=F32),
        sums[1] + lax.dot_general(p_ref[:, CH - 64 :], high, NN, preferred_element_type=F32),
    ]


def kind_kernel(slots, stacked, summed, own_ref, p_ref, rows_ref, *rest):
    w_ref = rest[0] if slots else None
    sg_ref = rest[1] if slots and summed else None
    keep_ref, send_ref = rest[-3 - slots], rest[-2 - slots]
    if slots:
        out_ref = rest[-2]
        sums = [sg_ref[0], sg_ref[1]] if summed else [0.0, 0.0]
        sums = slot_sums(p_ref, w_ref, sums)
        for h in range(2):
            out_ref[h] = sums[h]
    grad_chunk(own_ref, p_ref[...], rows_ref, rest[-1], keep_ref, send_ref)


STACK = jax.ShapeDtypeStruct((RING, PART, WID), BF)
SUMS = jax.ShapeDtypeStruct((2, HALF, WID), F32)
ANY = pl.BlockSpec(memory_space=pl.ANY)


def kind_step(t, own, piece, rows, stacks, w=None, sg=None):
    slots, stacked, summed = w is not None, stacks is not None, sg is not None
    in_specs, args = [PACK_SPEC, ROW_SPEC], [piece, rows]
    if slots:
        in_specs, args = in_specs + [w_spec(t)], args + [w]
    aliases = {}
    if summed:
        aliases[len(args) + 1] = 2
        in_specs, args = in_specs + [ROW_SPEC], args + [sg]
    if stacked:
        aliases[len(args) + 1], aliases[len(args) + 2] = 0, 1
        in_specs, args = in_specs + [ANY, ANY], args + list(stacks)
    one = pl.BlockSpec((1, PART, WID), lambda i, own: (t, 0, 0))
    out = call(
        functools.partial(kind_kernel, slots, stacked, summed),
        "kind_step",
        in_specs,
        [one, one] + [ROW_SPEC] * slots,
        [STACK, STACK] + [SUMS] * slots,
        (2 if slots else 1) * PROD,
        6_000_000 if slots else 2_000_000,
        [pltpu.VMEM((CH, WID), F32)],
        aliases,
    )(own, *args)
    return out[:2], (out[2] if slots else None)


def slot_last_kernel(own_ref, pg_ref, pu_ref, wg_ref, wu_ref, sg_ref, o_ref, acc):
    sums = slot_sums(pg_ref, wg_ref, [sg_ref[0], sg_ref[1]])
    sums = slot_sums(pu_ref, wu_ref, sums)
    for h in range(2):
        acc[...] = sums[h]
        for s in range(EXPERTS // 2):
            o_ref[h * (EXPERTS // 2) + s] = acc[CAP * s : CAP * (s + 1), :].astype(BF)


def slot_last(t, own, pg, pu, wg, wu, sg):
    whole = lambda shape: pl.BlockSpec(shape, lambda i, own: (0,) * len(shape))
    return pl.pallas_call(
        slot_last_kernel,
        grid_spec=pltpu.PrefetchScalarGridSpec(
            num_scalar_prefetch=1,
            grid=(1,),
            in_specs=[whole((HALF, PACK))] * 2 + [w_spec(t)] * 2 + [whole((2, HALF, WID))],
            out_specs=whole((EXPERTS, CAP, WID)),
            scratch_shapes=[pltpu.VMEM((HALF, WID), F32)],
        ),
        out_shape=jax.ShapeDtypeStruct((EXPERTS, CAP, WID), BF),
        compiler_params=params(16),
        cost_estimate=cost(2 * PROD, 5_500_000),
        name="slot_last",
    )(own, pg, pu, wg, wu, sg)


def merge_kernel(own_ref, keep_ref, recv_ref, o_ref):
    for t in range(RING):
        place = pl.ds(pl.multiple_of(own_ref[t] * PART, PART), PART)
        total = keep_ref[t].astype(F32) + recv_ref[(RING - t) % RING].astype(F32)
        o_ref[place, :] = total.astype(BF)


def merge(own, stacks):
    keep, recv = stacks[0], lax.ppermute(stacks[1], "dp", [(0, 1), (1, 0)])
    whole = pl.BlockSpec((RING, PART, WID), lambda i, own: (0, 0, 0))
    return pl.pallas_call(
        merge_kernel,
        grid_spec=pltpu.PrefetchScalarGridSpec(
            num_scalar_prefetch=1,
            grid=(1,),
            in_specs=[whole, whole],
            out_specs=pl.BlockSpec((FF // 2, WID), lambda i, own: (0, 0)),
        ),
        out_shape=jax.ShapeDtypeStruct((FF // 2, WID), BF),
        compiler_params=params(),
        name="merge",
    )(own, keep, recv)[None]


def ring_hop(x):
    up = [(i, (i + 1) % RING) for i in range(RING)]
    down = [(RING + i, RING + (i - 1) % RING) for i in range(RING)]
    return lax.ppermute(x, ("dp", "etp"), up + down)


def tie(x, *after):
    return lax.optimization_barrier((x, *after))[0]


def exchange(x):
    return lax.all_to_all(x, "expert", split_axis=0, concat_axis=0, tiled=True)


def per_device(tokens_in, grad_output, routes, route_numer, w_gate, w_up, w_down):
    dp, z = lax.axis_index("dp"), lax.axis_index("etp")
    sign = 1 - 2 * dp
    hops = jnp.arange(RING, dtype=jnp.int32)
    own = jnp.concatenate([(z - sign * hops) % RING, dp[None]]).astype(jnp.int32)
    wg, wu, wd = (w.reshape(2, FF // 2, WID) for w in (w_gate, w_up, w_down))
    rt, nt = routes.T, route_numer.T

    x_recv = exchange(build_slots(rt, None, tokens_in))
    g_send = build_slots(rt, nt, grad_output)
    g_recv = exchange(g_send)
    xs = tie(x_recv, g_send).reshape(2, HALF, WID)

    gate, up = rs_step(1, own, xs, wg, None), rs_step(1, own, xs, wu, None)
    back = None
    for t in range(2, RING + 1):
        gate, up = ring_hop(gate), ring_hop(up)
        if t > 2:
            back_recv = ring_hop(back)
            gate = tie(gate, back)
        if t < RING:
            gate, up = rs_step(t, own, xs, wg, gate), rs_step(t, own, xs, wu, up)
        else:
            gate_pre, up_pre, hid = hidden_step(own, xs, wg, wu, gate, up)
        if t == 2:
            gs = tie(g_recv, gate, up).reshape(2, HALF, WID)
            back = rs_step(1, own, gs, wd, None)
        else:
            back_recv = tie(back_recv, *((gate, up) if t < RING else (hid,)))
            back = rs_step(t - 1, own, gs, wd, back_recv)
    back_recv = ring_hop(back)

    hids, h_stack = [hid], None

    def hid_turn(last=False):
        nonlocal h_stack
        piece = hids[-1]
        if not last:
            hids.append(ring_hop(piece if h_stack is None else tie(piece, h_stack[0])))
        h_stack, _ = kind_step(len(hids) - 2 + last, own, piece, gs, h_stack)

    hid_turn()
    pg, pu = grads_step(own, gs, wd, back_recv, gate_pre, up_pre)
    pg = tie(pg, hids[-1])

    g_stack = u_stack = sg = None
    for t in range(RING):
        if t > 0:
            pg, pu = ring_hop(tie(pg, *g_done)), ring_hop(tie(pu, *u_done))
            if t < RING - 1:
                hid_turn()
            elif t == RING - 1:
                hid_turn(True)
        g_done = () if t == 0 else (g_stack[0],)
        u_done = () if t == 0 else (u_stack[0],)
        if t < RING - 1:
            g_stack, sg = kind_step(t, own, pg, xs, g_stack, wg, sg)
            u_stack, sg = kind_step(t, own, pu, xs, u_stack, wu, sg)
    pu = tie(pu, h_stack[0])
    slots = slot_last(t, own, pg, pu, wg, wu, sg)
    returned = exchange(slots)
    g_stack, _ = kind_step(t, own, tie(pg, slots), xs, g_stack)
    u_stack, _ = kind_step(t, own, tie(pu, slots), xs, u_stack)
    grad_input = gather_back(rt, returned)
    return (grad_input, merge(own, g_stack), merge(own, u_stack), merge(own, h_stack))


def solution(mesh):
    placed = (
        P(("dp", "expert"), "etp"),
        P(("dp", "expert"), "etp"),
        P(("dp", "expert"), None),
        P(("dp", "expert"), None),
        P("expert", None, "etp"),
        P("expert", None, "etp"),
        P("expert", None, "etp"),
    )
    return jax.shard_map(
        per_device,
        mesh=mesh,
        in_specs=placed,
        out_specs=(
            P(("dp", "expert"), "etp"),
            P("expert", "dp", "etp"),
            P("expert", "dp", "etp"),
            P("expert", "dp", "etp"),
        ),
        check_vma=False,
    )
```

```python
import functools
import jax
import jax.numpy as jnp
from jax import lax
from jax.experimental import pallas as pl
from jax.experimental.pallas import tpu as pltpu
from jax.sharding import PartitionSpec as P

EXPERTS = 16
CAP = 66
PAD = 72
TOK = 128
RING = 8
ROWS = EXPERTS * CAP
HALF = ROWS // 2
WID = 512
FF = 1536
PART = FF // (2 * RING)
CH = 2 * PART
PACK = 2 * CH
TILE = 176
STEPS = HALF // TILE
F32 = jnp.float32
BF = jnp.bfloat16
NT = (((1,), (1,)), ((), ()))
NN = (((1,), (0,)), ((), ()))
TN = (((0,), (0,)), ((), ()))


def params(mib=12):
    return pltpu.CompilerParams(
        dimension_semantics=("arbitrary",), vmem_limit_bytes=mib * 1024 * 1024
    )


def cost(flops, nbytes):
    return pl.CostEstimate(flops=flops, bytes_accessed=nbytes, transcendentals=0)


def one_hot(first, count, rt):
    ids = lax.broadcasted_iota(jnp.int32, (count, 8, TOK), 0) + first
    match = jnp.where(rt[None] == ids, 1.0, 0.0)
    member = jnp.sum(match, axis=1)
    below = lax.broadcasted_iota(jnp.int32, (TOK, TOK), 0) < lax.broadcasted_iota(
        jnp.int32, (TOK, TOK), 1
    )
    before = lax.dot_general(
        member.astype(BF), jnp.where(below, 1.0, 0.0).astype(BF), NN, preferred_element_type=F32
    )
    place = jnp.where(member > 0.0, before, -1.0)
    slot = lax.broadcasted_iota(jnp.int32, (count, PAD, TOK), 1).astype(F32)
    return jnp.where(place[:, None, :] == slot, 1.0, 0.0), match


def slots_kernel(rt_ref, nt_ref, v_ref, o_ref):
    count = o_ref.shape[0]
    pick, match = one_hot(pl.program_id(0) * count, count, rt_ref[...])
    flat = pick.reshape(count * PAD, TOK).astype(BF)
    rows = lax.dot_general(flat, v_ref[...], NN, preferred_element_type=F32)
    rows = rows.reshape(count, PAD, WID)
    if nt_ref is not None:
        num = nt_ref[...].astype(F32)
        share = num / jnp.sum(num, axis=0, keepdims=True)
        weight = jnp.sum(match * share[None], axis=1)
        rows = rows * jnp.sum(pick * weight[:, None, :], axis=2, keepdims=True)
    o_ref[...] = rows[:, :CAP].astype(BF)


def plain_slots_kernel(rt_ref, v_ref, o_ref):
    slots_kernel(rt_ref, None, v_ref, o_ref)


def build_slots(rt, nt, values):
    count = 8
    whole = lambda x: pl.BlockSpec(x.shape, lambda i: (0, 0))
    args = [rt, values] if nt is None else [rt, nt, values]
    return pl.pallas_call(
        plain_slots_kernel if nt is None else slots_kernel,
        grid=(EXPERTS // count,),
        in_specs=[whole(x) for x in args],
        out_specs=pl.BlockSpec((count, CAP, WID), lambda i: (i, 0, 0)),
        out_shape=jax.ShapeDtypeStruct((EXPERTS, CAP, WID), BF),
        compiler_params=params(56),
        cost_estimate=cost(2 * EXPERTS * PAD * TOK * WID, 1_500_000),
        name="build_slots",
    )(*args)


def regroup_kernel(v_ref, o_ref, wide):
    for s in range(EXPERTS // 2):
        wide[CAP * s : CAP * (s + 1), :] = v_ref[s].astype(F32)
    o_ref[0] = wide[...].astype(BF)


def regroup(values):
    return pl.pallas_call(
        regroup_kernel,
        grid=(2,),
        in_specs=[pl.BlockSpec((EXPERTS // 2, CAP, WID), lambda i: (i, 0, 0))],
        out_specs=pl.BlockSpec((1, HALF, WID), lambda i: (i, 0, 0)),
        out_shape=jax.ShapeDtypeStruct((2, HALF, WID), BF),
        scratch_shapes=[pltpu.VMEM((HALF, WID), F32)],
        compiler_params=params(),
        cost_estimate=cost(1000, 2_200_000),
        name="regroup",
    )(values)


def back_kernel(rt_ref, v_ref, o_ref, acc, wide):
    count = v_ref.shape[0]
    pick, _ = one_hot(pl.program_id(0) * count, count, rt_ref[...])
    wide[...] = jnp.zeros_like(wide)
    wide[:, :CAP, :] = v_ref[...].astype(F32)
    part = lax.dot_general(
        pick.reshape(count * PAD, TOK).astype(BF),
        wide[...].reshape(count * PAD, WID).astype(BF),
        TN,
        preferred_element_type=F32,
    )

    @pl.when(pl.program_id(0) == 0)
    def _():
        acc[...] = part

    @pl.when(pl.program_id(0) > 0)
    def _():
        acc[...] += part

    @pl.when(pl.program_id(0) == pl.num_programs(0) - 1)
    def _():
        o_ref[...] = acc[...].astype(BF)


def gather_back(rt, values):
    count = 8
    return pl.pallas_call(
        back_kernel,
        grid=(EXPERTS // count,),
        in_specs=[
            pl.BlockSpec((8, TOK), lambda i: (0, 0)),
            pl.BlockSpec((count, CAP, WID), lambda i: (i, 0, 0)),
        ],
        out_specs=pl.BlockSpec((TOK, WID), lambda i: (0, 0)),
        out_shape=jax.ShapeDtypeStruct((TOK, WID), BF),
        scratch_shapes=[pltpu.VMEM((TOK, WID), F32), pltpu.VMEM((count, PAD, WID), F32)],
        compiler_params=params(),
        name="gather_back",
    )(rt, values)


def padded(w_ref):
    w = w_ref[...].reshape(CH, WID)
    zero = jnp.zeros((64, WID), BF)
    return jnp.concatenate([w, zero], axis=0), jnp.concatenate([zero, w], axis=0)


def partial_sums(rows_ref, w_ref, recv_ref):
    low, high = padded(w_ref)
    d1 = lax.dot_general(rows_ref[0], low, NT, preferred_element_type=F32)
    d2 = lax.dot_general(rows_ref[1], high, NT, preferred_element_type=F32)
    blocks = [d1[:, :128], d1[:, 128:] + d2[:, :128], d2[:, 128:]]
    if recv_ref is not None:
        blocks = [b + recv_ref[:, 128 * i : 128 * (i + 1)].astype(F32) for i, b in enumerate(blocks)]
    return blocks


def rs_kernel(first, own_ref, rows_ref, w_ref, *rest):
    recv_ref, o_ref = (None, rest[0]) if first else rest
    for i, b in enumerate(partial_sums(rows_ref, w_ref, recv_ref)):
        o_ref[:, 128 * i : 128 * (i + 1)] = b.astype(BF)


ROW_SPEC = pl.BlockSpec((2, TILE, WID), lambda i, own: (0, i, 0))
PACK_SPEC = pl.BlockSpec((TILE, PACK), lambda i, own: (i, 0))
PACK_BF = jax.ShapeDtypeStruct((HALF, PACK), BF)
PACK_F32 = jax.ShapeDtypeStruct((HALF, PACK), F32)


def w_spec(t):
    return pl.BlockSpec((2, PART, WID), lambda i, own: (0, own[t], 0))


def call(kernel, name, in_specs, out_specs, out_shape, flops, nbytes, scratch=(), aliases=None):
    return pl.pallas_call(
        kernel,
        grid_spec=pltpu.PrefetchScalarGridSpec(
            num_scalar_prefetch=1,
            grid=(STEPS,),
            in_specs=in_specs,
            out_specs=out_specs,
            scratch_shapes=scratch,
        ),
        out_shape=out_shape,
        input_output_aliases=aliases or {},
        compiler_params=params(),
        cost_estimate=cost(flops, nbytes),
        name=name,
    )


PROD = 2 * ROWS * CH * WID


def rs_step(t, own, rows, w, recv):
    first = recv is None
    return call(
        functools.partial(rs_kernel, first),
        "rs_step",
        [ROW_SPEC, w_spec(t)] + ([] if first else [PACK_SPEC]),
        PACK_SPEC,
        PACK_BF,
        PROD,
        2_500_000,
    )(own, rows, w, *(() if first else (recv,)))


def hidden_kernel(own_ref, rows_ref, wg_ref, wu_ref, rg_ref, ru_ref, gp_ref, up_ref, h_ref):
    gate = partial_sums(rows_ref, wg_ref, rg_ref)
    up = partial_sums(rows_ref, wu_ref, ru_ref)
    for i in range(3):
        lanes = slice(128 * i, 128 * (i + 1))
        gp_ref[:, lanes] = gate[i]
        up_ref[:, lanes] = up[i]
        h_ref[:, lanes] = (gate[i] * jax.nn.sigmoid(gate[i]) * up[i]).astype(BF)


def hidden_step(own, rows, wg, wu, rg, ru):
    return call(
        hidden_kernel,
        "hidden_step",
        [ROW_SPEC, w_spec(0), w_spec(0), PACK_SPEC, PACK_SPEC],
        [PACK_SPEC] * 3,
        [PACK_F32, PACK_F32, PACK_BF],
        2 * PROD,
        5_000_000,
    )(own, rows, wg, wu, rg, ru)


def grads_kernel(own_ref, rows_ref, w_ref, r_ref, gp_ref, up_ref, gg_ref, gu_ref):
    grad = partial_sums(rows_ref, w_ref, r_ref)
    for i in range(3):
        lanes = slice(128 * i, 128 * (i + 1))
        gate, up = gp_ref[:, lanes], up_ref[:, lanes]
        sig = jax.nn.sigmoid(gate)
        gg_ref[:, lanes] = (grad[i] * up * sig * (1.0 + gate * (1.0 - sig))).astype(BF)
        gu_ref[:, lanes] = (grad[i] * (gate * sig)).astype(BF)


def grads_step(own, rows, w, recv, gate, up):
    return call(
        grads_kernel,
        "grads_step",
        [ROW_SPEC, w_spec(0), PACK_SPEC, PACK_SPEC, PACK_SPEC],
        [PACK_SPEC] * 2,
        [PACK_BF] * 2,
        PROD,
        5_000_000,
    )(own, rows, w, recv, gate, up)


def weight_grad(piece, rows_ref):
    a = lax.dot_general(piece[:, : CH + 64], rows_ref[0], TN, preferred_element_type=F32)
    b = lax.dot_general(piece[:, CH - 64 :], rows_ref[1], TN, preferred_element_type=F32)
    return a[:CH] + b[64:]


def grad_chunk(own_ref, piece, rows_ref, acc, keep_ref, send_ref):
    part = weight_grad(piece, rows_ref)

    @pl.when(pl.program_id(0) == 0)
    def _():
        acc[...] = part

    @pl.when(pl.program_id(0) > 0)
    def _():
        acc[...] += part

    @pl.when(pl.program_id(0) == STEPS - 1)
    def _():
        mine = own_ref[RING] == 0
        low, high = acc[:PART].astype(BF), acc[PART:].astype(BF)
        keep_ref[0] = jnp.where(mine, low, high)
        send_ref[0] = jnp.where(mine, high, low)


def slot_sums(p_ref, w_ref, sums):
    low, high = padded(w_ref)
    return [
        sums[0] + lax.dot_general(p_ref[:, : CH + 64], low, NN, preferred_element_type=F32),
        sums[1] + lax.dot_general(p_ref[:, CH - 64 :], high, NN, preferred_element_type=F32),
    ]


def kind_kernel(slots, stacked, summed, own_ref, p_ref, rows_ref, *rest):
    w_ref = rest[0] if slots else None
    sg_ref = rest[1] if slots and summed else None
    keep_ref, send_ref = rest[-3 - slots], rest[-2 - slots]
    if slots:
        out_ref = rest[-2]
        sums = [sg_ref[0], sg_ref[1]] if summed else [0.0, 0.0]
        sums = slot_sums(p_ref, w_ref, sums)
        for h in range(2):
            out_ref[h] = sums[h]
    grad_chunk(own_ref, p_ref[...], rows_ref, rest[-1], keep_ref, send_ref)


STACK = jax.ShapeDtypeStruct((RING, PART, WID), BF)
SUMS = jax.ShapeDtypeStruct((2, HALF, WID), F32)
ANY = pl.BlockSpec(memory_space=pl.ANY)


def kind_step(t, own, piece, rows, stacks, w=None, sg=None):
    slots, stacked, summed = w is not None, stacks is not None, sg is not None
    in_specs, args = [PACK_SPEC, ROW_SPEC], [piece, rows]
    if slots:
        in_specs, args = in_specs + [w_spec(t)], args + [w]
    aliases = {}
    if summed:
        aliases[len(args) + 1] = 2
        in_specs, args = in_specs + [ROW_SPEC], args + [sg]
    if stacked:
        aliases[len(args) + 1], aliases[len(args) + 2] = 0, 1
        in_specs, args = in_specs + [ANY, ANY], args + list(stacks)
    one = pl.BlockSpec((1, PART, WID), lambda i, own: (t, 0, 0))
    out = call(
        functools.partial(kind_kernel, slots, stacked, summed),
        "kind_step",
        in_specs,
        [one, one] + [ROW_SPEC] * slots,
        [STACK, STACK] + [SUMS] * slots,
        (2 if slots else 1) * PROD,
        6_000_000 if slots else 2_000_000,
        [pltpu.VMEM((CH, WID), F32)],
        aliases,
    )(own, *args)
    return out[:2], (out[2] if slots else None)


def slot_last_kernel(own_ref, pg_ref, pu_ref, wg_ref, wu_ref, sg_ref, o_ref, acc):
    sums = slot_sums(pg_ref, wg_ref, [sg_ref[0], sg_ref[1]])
    sums = slot_sums(pu_ref, wu_ref, sums)
    for h in range(2):
        acc[...] = sums[h]
        for s in range(EXPERTS // 2):
            o_ref[h * (EXPERTS // 2) + s] = acc[CAP * s : CAP * (s + 1), :].astype(BF)


def slot_last(t, own, pg, pu, wg, wu, sg):
    whole = lambda shape: pl.BlockSpec(shape, lambda i, own: (0,) * len(shape))
    return pl.pallas_call(
        slot_last_kernel,
        grid_spec=pltpu.PrefetchScalarGridSpec(
            num_scalar_prefetch=1,
            grid=(1,),
            in_specs=[whole((HALF, PACK))] * 2 + [w_spec(t)] * 2 + [whole((2, HALF, WID))],
            out_specs=whole((EXPERTS, CAP, WID)),
            scratch_shapes=[pltpu.VMEM((HALF, WID), F32)],
        ),
        out_shape=jax.ShapeDtypeStruct((EXPERTS, CAP, WID), BF),
        compiler_params=params(16),
        cost_estimate=cost(2 * PROD, 5_500_000),
        name="slot_last",
    )(own, pg, pu, wg, wu, sg)


def merge_kernel(own_ref, keep_ref, recv_ref, o_ref):
    for t in range(RING):
        place = pl.ds(pl.multiple_of(own_ref[t] * PART, PART), PART)
        total = keep_ref[t].astype(F32) + recv_ref[(RING - t) % RING].astype(F32)
        o_ref[place, :] = total.astype(BF)


def merge(own, stacks):
    keep, recv = stacks[0], lax.ppermute(stacks[1], "dp", [(0, 1), (1, 0)])
    whole = pl.BlockSpec((RING, PART, WID), lambda i, own: (0, 0, 0))
    return pl.pallas_call(
        merge_kernel,
        grid_spec=pltpu.PrefetchScalarGridSpec(
            num_scalar_prefetch=1,
            grid=(1,),
            in_specs=[whole, whole],
            out_specs=pl.BlockSpec((FF // 2, WID), lambda i, own: (0, 0)),
        ),
        out_shape=jax.ShapeDtypeStruct((FF // 2, WID), BF),
        compiler_params=params(),
        name="merge",
    )(own, keep, recv)[None]


def ring_hop(x):
    up = [(i, (i + 1) % RING) for i in range(RING)]
    down = [(RING + i, RING + (i - 1) % RING) for i in range(RING)]
    return lax.ppermute(x, ("dp", "etp"), up + down)


def tie(x, *after):
    return lax.optimization_barrier((x, *after))[0]


def exchange(x):
    return lax.all_to_all(x, "expert", split_axis=0, concat_axis=0, tiled=True)


def per_device(tokens_in, grad_output, routes, route_numer, w_gate, w_up, w_down):
    dp, z = lax.axis_index("dp"), lax.axis_index("etp")
    sign = 1 - 2 * dp
    hops = jnp.arange(RING, dtype=jnp.int32)
    own = jnp.concatenate([(z - sign * hops) % RING, dp[None]]).astype(jnp.int32)
    wg, wu, wd = (w.reshape(2, FF // 2, WID) for w in (w_gate, w_up, w_down))
    rt, nt = routes.T, route_numer.T

    x_recv = exchange(build_slots(rt, None, tokens_in))
    g_send = build_slots(rt, nt, grad_output)
    g_recv = exchange(g_send)
    xs = tie(x_recv, g_send).reshape(2, HALF, WID)

    gate, up = rs_step(1, own, xs, wg, None), rs_step(1, own, xs, wu, None)
    back = None
    for t in range(2, RING + 1):
        gate, up = ring_hop(gate), ring_hop(up)
        if t > 2:
            back_recv = ring_hop(back)
            gate = tie(gate, back)
        if t < RING:
            gate, up = rs_step(t, own, xs, wg, gate), rs_step(t, own, xs, wu, up)
        else:
            gate_pre, up_pre, hid = hidden_step(own, xs, wg, wu, gate, up)
        if t == 2:
            gs = regroup(tie(g_recv, gate, up))
            back = rs_step(1, own, gs, wd, None)
        else:
            back_recv = tie(back_recv, *((gate, up) if t < RING else (hid,)))
            back = rs_step(t - 1, own, gs, wd, back_recv)
    back_recv = ring_hop(back)

    hids, h_stacks = [hid], []

    def hid_turn(last=False):
        t, piece = len(hids) - 1, hids[-1]
        if not last:
            hids.append(ring_hop(tie(piece, h_stacks[t - 3][0]) if t >= 3 else piece))
        h_stacks.append(kind_step(t, own, piece, gs, h_stacks[-1] if t else None)[0])

    hid_turn()
    hid_turn()
    pg, pu = grads_step(own, gs, wd, back_recv, gate_pre, up_pre)
    pg = tie(pg, hids[-1])
    pu = tie(pu, pg)

    g_stack = u_stack = sg = None
    for t in range(RING):
        if t > 0:
            pg, pu = ring_hop(tie(pg, *g_done)), ring_hop(tie(pu, *u_done))
            if t < RING - 2:
                hid_turn()
            elif t == RING - 2:
                hid_turn(True)
        g_done = () if t == 0 else (g_stack[0],)
        u_done = () if t == 0 else (u_stack[0],)
        if t < RING - 1:
            g_stack, sg = kind_step(t, own, pg, xs, g_stack, wg, sg)
            u_stack, sg = kind_step(t, own, pu, xs, u_stack, wu, sg)
    pu = tie(pu, h_stacks[-1][0])
    slots = slot_last(t, own, pg, pu, wg, wu, sg)
    returned = exchange(slots)
    g_stack, _ = kind_step(t, own, tie(pg, slots), xs, g_stack)
    u_stack, _ = kind_step(t, own, tie(pu, slots), xs, u_stack)
    grad_input = gather_back(rt, returned)
    return (grad_input, merge(own, g_stack), merge(own, u_stack), merge(own, h_stacks[-1]))


def solution(mesh):
    placed = (
        P(("dp", "expert"), "etp"),
        P(("dp", "expert"), "etp"),
        P(("dp", "expert"), None),
        P(("dp", "expert"), None),
        P("expert", None, "etp"),
        P("expert", None, "etp"),
        P("expert", None, "etp"),
    )
    return jax.shard_map(
        per_device,
        mesh=mesh,
        in_specs=placed,
        out_specs=(
            P(("dp", "expert"), "etp"),
            P("expert", "dp", "etp"),
            P("expert", "dp", "etp"),
            P("expert", "dp", "etp"),
        ),
        check_vma=False,
    )
```

```python
import functools
import jax
import jax.numpy as jnp
from jax import lax
from jax.experimental import pallas as pl
from jax.experimental.pallas import tpu as pltpu
from jax.sharding import PartitionSpec as P

EXPERTS = 16
CAP = 66
PAD = 72
TOK = 128
RING = 8
ROWS = EXPERTS * CAP
HALF = ROWS // 2
WID = 512
FF = 1536
PART = FF // (2 * RING)
CH = 2 * PART
PACK = 2 * CH
TILE = 528
STEPS = HALF // TILE
F32 = jnp.float32
BF = jnp.bfloat16
NT = (((1,), (1,)), ((), ()))
NN = (((1,), (0,)), ((), ()))
TN = (((0,), (0,)), ((), ()))


def params(mib=20):
    return pltpu.CompilerParams(
        dimension_semantics=("arbitrary",), vmem_limit_bytes=mib * 1024 * 1024
    )


def cost(flops, nbytes):
    return pl.CostEstimate(flops=flops, bytes_accessed=nbytes, transcendentals=0)


def one_hot(first, count, rt):
    ids = lax.broadcasted_iota(jnp.int32, (count, 8, TOK), 0) + first
    match = jnp.where(rt[None] == ids, 1.0, 0.0)
    member = jnp.sum(match, axis=1)
    below = lax.broadcasted_iota(jnp.int32, (TOK, TOK), 0) < lax.broadcasted_iota(
        jnp.int32, (TOK, TOK), 1
    )
    before = lax.dot_general(
        member.astype(BF), jnp.where(below, 1.0, 0.0).astype(BF), NN, preferred_element_type=F32
    )
    place = jnp.where(member > 0.0, before, -1.0)
    slot = lax.broadcasted_iota(jnp.int32, (count, PAD, TOK), 1).astype(F32)
    return jnp.where(place[:, None, :] == slot, 1.0, 0.0), match


def slots_kernel(rt_ref, nt_ref, v_ref, o_ref):
    count = o_ref.shape[0]
    pick, match = one_hot(pl.program_id(0) * count, count, rt_ref[...])
    flat = pick.reshape(count * PAD, TOK).astype(BF)
    rows = lax.dot_general(flat, v_ref[...], NN, preferred_element_type=F32)
    rows = rows.reshape(count, PAD, WID)
    if nt_ref is not None:
        num = nt_ref[...].astype(F32)
        share = num / jnp.sum(num, axis=0, keepdims=True)
        weight = jnp.sum(match * share[None], axis=1)
        rows = rows * jnp.sum(pick * weight[:, None, :], axis=2, keepdims=True)
    o_ref[...] = rows[:, :CAP].astype(BF)


def plain_slots_kernel(rt_ref, v_ref, o_ref):
    slots_kernel(rt_ref, None, v_ref, o_ref)


def build_slots(rt, nt, values):
    count = 8
    whole = lambda x: pl.BlockSpec(x.shape, lambda i: (0, 0))
    args = [rt, values] if nt is None else [rt, nt, values]
    return pl.pallas_call(
        plain_slots_kernel if nt is None else slots_kernel,
        grid=(EXPERTS // count,),
        in_specs=[whole(x) for x in args],
        out_specs=pl.BlockSpec((count, CAP, WID), lambda i: (i, 0, 0)),
        out_shape=jax.ShapeDtypeStruct((EXPERTS, CAP, WID), BF),
        compiler_params=params(56),
        cost_estimate=cost(2 * EXPERTS * PAD * TOK * WID, 1_500_000),
        name="build_slots",
    )(*args)


def regroup_kernel(v_ref, o_ref, wide):
    for s in range(EXPERTS // 2):
        wide[CAP * s : CAP * (s + 1), :] = v_ref[s].astype(F32)
    o_ref[0] = wide[...].astype(BF)


def regroup(values):
    return pl.pallas_call(
        regroup_kernel,
        grid=(2,),
        in_specs=[pl.BlockSpec((EXPERTS // 2, CAP, WID), lambda i: (i, 0, 0))],
        out_specs=pl.BlockSpec((1, HALF, WID), lambda i: (i, 0, 0)),
        out_shape=jax.ShapeDtypeStruct((2, HALF, WID), BF),
        scratch_shapes=[pltpu.VMEM((HALF, WID), F32)],
        compiler_params=params(),
        cost_estimate=cost(1000, 2_200_000),
        name="regroup",
    )(values)


def back_kernel(rt_ref, v_ref, o_ref, acc, wide):
    count = v_ref.shape[0]
    pick, _ = one_hot(pl.program_id(0) * count, count, rt_ref[...])
    wide[...] = jnp.zeros_like(wide)
    wide[:, :CAP, :] = v_ref[...].astype(F32)
    part = lax.dot_general(
        pick.reshape(count * PAD, TOK).astype(BF),
        wide[...].reshape(count * PAD, WID).astype(BF),
        TN,
        preferred_element_type=F32,
    )

    @pl.when(pl.program_id(0) == 0)
    def _():
        acc[...] = part

    @pl.when(pl.program_id(0) > 0)
    def _():
        acc[...] += part

    @pl.when(pl.program_id(0) == pl.num_programs(0) - 1)
    def _():
        o_ref[...] = acc[...].astype(BF)


def gather_back(rt, values):
    count = 8
    return pl.pallas_call(
        back_kernel,
        grid=(EXPERTS // count,),
        in_specs=[
            pl.BlockSpec((8, TOK), lambda i: (0, 0)),
            pl.BlockSpec((count, CAP, WID), lambda i: (i, 0, 0)),
        ],
        out_specs=pl.BlockSpec((TOK, WID), lambda i: (0, 0)),
        out_shape=jax.ShapeDtypeStruct((TOK, WID), BF),
        scratch_shapes=[pltpu.VMEM((TOK, WID), F32), pltpu.VMEM((count, PAD, WID), F32)],
        compiler_params=params(),
        name="gather_back",
    )(rt, values)


def padded(w_ref):
    w = w_ref[...].reshape(CH, WID)
    zero = jnp.zeros((64, WID), BF)
    return jnp.concatenate([w, zero], axis=0), jnp.concatenate([zero, w], axis=0)


def partial_sums(rows_ref, w_ref, recv_ref):
    low, high = padded(w_ref)
    d1 = lax.dot_general(rows_ref[0], low, NT, preferred_element_type=F32)
    d2 = lax.dot_general(rows_ref[1], high, NT, preferred_element_type=F32)
    blocks = [d1[:, :128], d1[:, 128:] + d2[:, :128], d2[:, 128:]]
    if recv_ref is not None:
        blocks = [b + recv_ref[:, 128 * i : 128 * (i + 1)].astype(F32) for i, b in enumerate(blocks)]
    return blocks


def rs_kernel(first, own_ref, rows_ref, w_ref, *rest):
    recv_ref, o_ref = (None, rest[0]) if first else rest
    for i, b in enumerate(partial_sums(rows_ref, w_ref, recv_ref)):
        o_ref[:, 128 * i : 128 * (i + 1)] = b.astype(BF)


ROW_SPEC = pl.BlockSpec((2, TILE, WID), lambda i, own: (0, i, 0))
PACK_SPEC = pl.BlockSpec((TILE, PACK), lambda i, own: (i, 0))
CHUNK_SPEC = pl.BlockSpec((2, PART, WID), lambda i, own: (0, 0, 0))
PACK_BF = jax.ShapeDtypeStruct((HALF, PACK), BF)
PACK_F32 = jax.ShapeDtypeStruct((HALF, PACK), F32)


def w_spec(t):
    return pl.BlockSpec((2, PART, WID), lambda i, own: (0, own[t], 0))


def call(kernel, name, in_specs, out_specs, out_shape, flops, nbytes, scratch=(), aliases=None):
    return pl.pallas_call(
        kernel,
        grid_spec=pltpu.PrefetchScalarGridSpec(
            num_scalar_prefetch=1,
            grid=(STEPS,),
            in_specs=in_specs,
            out_specs=out_specs,
            scratch_shapes=scratch,
        ),
        out_shape=out_shape,
        input_output_aliases=aliases or {},
        compiler_params=params(),
        cost_estimate=cost(flops, nbytes),
        name=name,
    )


PROD = 2 * ROWS * CH * WID


def rs_step(t, own, rows, w, recv):
    first = recv is None
    return call(
        functools.partial(rs_kernel, first),
        "rs_step",
        [ROW_SPEC, CHUNK_SPEC if first else w_spec(t)] + ([] if first else [PACK_SPEC]),
        PACK_SPEC,
        PACK_BF,
        PROD,
        2_500_000,
    )(own, rows, w, *(() if first else (recv,)))


def hidden_kernel(own_ref, rows_ref, wg_ref, wu_ref, rg_ref, ru_ref, gp_ref, up_ref, h_ref):
    gate = partial_sums(rows_ref, wg_ref, rg_ref)
    up = partial_sums(rows_ref, wu_ref, ru_ref)
    for i in range(3):
        lanes = slice(128 * i, 128 * (i + 1))
        gp_ref[:, lanes] = gate[i]
        up_ref[:, lanes] = up[i]
        h_ref[:, lanes] = (gate[i] * jax.nn.sigmoid(gate[i]) * up[i]).astype(BF)


def hidden_step(own, rows, wg, wu, rg, ru):
    return call(
        hidden_kernel,
        "hidden_step",
        [ROW_SPEC, w_spec(0), w_spec(0), PACK_SPEC, PACK_SPEC],
        [PACK_SPEC] * 3,
        [PACK_F32, PACK_F32, PACK_BF],
        2 * PROD,
        5_000_000,
    )(own, rows, wg, wu, rg, ru)


def grads_kernel(own_ref, rows_ref, w_ref, r_ref, gp_ref, up_ref, gg_ref, gu_ref):
    grad = partial_sums(rows_ref, w_ref, r_ref)
    for i in range(3):
        lanes = slice(128 * i, 128 * (i + 1))
        gate, up = gp_ref[:, lanes], up_ref[:, lanes]
        sig = jax.nn.sigmoid(gate)
        gg_ref[:, lanes] = (grad[i] * up * sig * (1.0 + gate * (1.0 - sig))).astype(BF)
        gu_ref[:, lanes] = (grad[i] * (gate * sig)).astype(BF)


def grads_step(own, rows, w, recv, gate, up):
    return call(
        grads_kernel,
        "grads_step",
        [ROW_SPEC, w_spec(0), PACK_SPEC, PACK_SPEC, PACK_SPEC],
        [PACK_SPEC] * 2,
        [PACK_BF] * 2,
        PROD,
        5_000_000,
    )(own, rows, w, recv, gate, up)


def weight_grad(piece, rows_ref):
    a = lax.dot_general(piece[:, : CH + 64], rows_ref[0], TN, preferred_element_type=F32)
    b = lax.dot_general(piece[:, CH - 64 :], rows_ref[1], TN, preferred_element_type=F32)
    return a[:CH] + b[64:]


def grad_chunk(own_ref, piece, rows_ref, acc, keep_ref, send_ref):
    part = weight_grad(piece, rows_ref)

    @pl.when(pl.program_id(0) == 0)
    def _():
        acc[...] = part

    @pl.when(pl.program_id(0) > 0)
    def _():
        acc[...] += part

    @pl.when(pl.program_id(0) == STEPS - 1)
    def _():
        mine = own_ref[RING] == 0
        low, high = acc[:PART].astype(BF), acc[PART:].astype(BF)
        keep_ref[0] = jnp.where(mine, low, high)
        send_ref[0] = jnp.where(mine, high, low)


def slot_sums(p_ref, w_ref, sums):
    low, high = padded(w_ref)
    return [
        sums[0] + lax.dot_general(p_ref[:, : CH + 64], low, NN, preferred_element_type=F32),
        sums[1] + lax.dot_general(p_ref[:, CH - 64 :], high, NN, preferred_element_type=F32),
    ]


def kind_kernel(slots, stacked, summed, own_ref, p_ref, rows_ref, *rest):
    w_ref = rest[0] if slots else None
    sg_ref = rest[1] if slots and summed else None
    keep_ref, send_ref = rest[-3 - slots], rest[-2 - slots]
    if slots:
        out_ref = rest[-2]
        sums = [sg_ref[0], sg_ref[1]] if summed else [0.0, 0.0]
        sums = slot_sums(p_ref, w_ref, sums)
        for h in range(2):
            out_ref[h] = sums[h]
    grad_chunk(own_ref, p_ref[...], rows_ref, rest[-1], keep_ref, send_ref)


STACK = jax.ShapeDtypeStruct((RING, PART, WID), BF)
SUMS = jax.ShapeDtypeStruct((2, HALF, WID), F32)
ANY = pl.BlockSpec(memory_space=pl.ANY)


def kind_step(t, own, piece, rows, stacks, w=None, sg=None):
    slots, stacked, summed = w is not None, stacks is not None, sg is not None
    in_specs, args = [PACK_SPEC, ROW_SPEC], [piece, rows]
    if slots:
        in_specs, args = in_specs + [w_spec(t)], args + [w]
    aliases = {}
    if summed:
        aliases[len(args) + 1] = 2
        in_specs, args = in_specs + [ROW_SPEC], args + [sg]
    if stacked:
        aliases[len(args) + 1], aliases[len(args) + 2] = 0, 1
        in_specs, args = in_specs + [ANY, ANY], args + list(stacks)
    one = pl.BlockSpec((1, PART, WID), lambda i, own: (t, 0, 0))
    out = call(
        functools.partial(kind_kernel, slots, stacked, summed),
        "kind_step",
        in_specs,
        [one, one] + [ROW_SPEC] * slots,
        [STACK, STACK] + [SUMS] * slots,
        (2 if slots else 1) * PROD,
        6_000_000 if slots else 2_000_000,
        [pltpu.VMEM((CH, WID), F32)],
        aliases,
    )(own, *args)
    return out[:2], (out[2] if slots else None)


def slot_last_kernel(own_ref, p_ref, w_ref, sg_ref, o_ref, acc):
    sums = slot_sums(p_ref, w_ref, [sg_ref[0], sg_ref[1]])
    for h in range(2):
        acc[...] = sums[h]
        for s in range(EXPERTS // 2):
            o_ref[h * (EXPERTS // 2) + s] = acc[CAP * s : CAP * (s + 1), :].astype(BF)


def slot_last(t, own, piece, w, sg):
    whole = lambda shape: pl.BlockSpec(shape, lambda i, own: (0,) * len(shape))
    return pl.pallas_call(
        slot_last_kernel,
        grid_spec=pltpu.PrefetchScalarGridSpec(
            num_scalar_prefetch=1,
            grid=(1,),
            in_specs=[whole((HALF, PACK)), w_spec(t), whole((2, HALF, WID))],
            out_specs=whole((EXPERTS, CAP, WID)),
            scratch_shapes=[pltpu.VMEM((HALF, WID), F32)],
        ),
        out_shape=jax.ShapeDtypeStruct((EXPERTS, CAP, WID), BF),
        compiler_params=params(16),
        cost_estimate=cost(PROD, 4_500_000),
        name="slot_last",
    )(own, piece, w, sg)


def merge_kernel(own_ref, keep_ref, recv_ref, o_ref):
    for t in range(RING):
        place = pl.ds(pl.multiple_of(own_ref[t] * PART, PART), PART)
        total = keep_ref[t].astype(F32) + recv_ref[(RING - t) % RING].astype(F32)
        o_ref[place, :] = total.astype(BF)


def merge(own, stacks):
    keep, recv = stacks[0], lax.ppermute(stacks[1], "dp", [(0, 1), (1, 0)])
    whole = pl.BlockSpec((RING, PART, WID), lambda i, own: (0, 0, 0))
    return pl.pallas_call(
        merge_kernel,
        grid_spec=pltpu.PrefetchScalarGridSpec(
            num_scalar_prefetch=1,
            grid=(1,),
            in_specs=[whole, whole],
            out_specs=pl.BlockSpec((FF // 2, WID), lambda i, own: (0, 0)),
        ),
        out_shape=jax.ShapeDtypeStruct((FF // 2, WID), BF),
        compiler_params=params(),
        name="merge",
    )(own, keep, recv)[None]


def ring_hop(x):
    up = [(i, (i + 1) % RING) for i in range(RING)]
    down = [(RING + i, RING + (i - 1) % RING) for i in range(RING)]
    return lax.ppermute(x, ("dp", "etp"), up + down)


def tie(x, *after):
    return lax.optimization_barrier((x, *after))[0]


def exchange(x):
    return lax.all_to_all(x, "expert", split_axis=0, concat_axis=0, tiled=True)


def per_device(tokens_in, grad_output, routes, route_numer, w_gate, w_up, w_down):
    dp, z = lax.axis_index("dp"), lax.axis_index("etp")
    sign = 1 - 2 * dp
    hops = jnp.arange(RING, dtype=jnp.int32)
    own = jnp.concatenate([(z - sign * hops) % RING, dp[None]]).astype(jnp.int32)
    wg, wu, wd = (w.reshape(2, FF // 2, WID) for w in (w_gate, w_up, w_down))
    rt, nt = routes.T, route_numer.T

    x_recv = exchange(build_slots(rt, None, tokens_in))
    g_send = build_slots(rt, nt, grad_output)
    g_recv = exchange(g_send)

    wg1, wu1, wd1 = (lax.dynamic_slice_in_dim(w, own[1] * PART, PART, 1) for w in (wg, wu, wd))
    xs = regroup(tie(x_recv, g_send, wd1))
    gate, up = rs_step(1, own, xs, wg1, None), rs_step(1, own, xs, wu1, None)
    back = None
    for t in range(2, RING + 1):
        gate, up = ring_hop(gate), ring_hop(up)
        if t > 2:
            back_recv = ring_hop(back)
            gate = tie(gate, back)
        if t < RING:
            gate, up = rs_step(t, own, xs, wg, gate), rs_step(t, own, xs, wu, up)
        else:
            gate_pre, up_pre, hid = hidden_step(own, xs, wg, wu, gate, up)
        if t == 2:
            gs = regroup(tie(g_recv, gate, up))
            back = rs_step(1, own, gs, wd1, None)
        else:
            back_recv = tie(back_recv, *((gate, up) if t < RING else (hid,)))
            back = rs_step(t - 1, own, gs, wd, back_recv)
    back_recv = ring_hop(back)

    hids, h_stacks = [hid], []

    def hid_turn(last=False):
        t, piece = len(hids) - 1, hids[-1]
        if not last:
            hids.append(ring_hop(tie(piece, h_stacks[t - 3][0]) if t >= 3 else piece))
        h_stacks.append(kind_step(t, own, piece, gs, h_stacks[-1] if t else None)[0])

    hid_turn()
    hid_turn()
    pg, pu = grads_step(own, gs, wd, back_recv, gate_pre, up_pre)
    pu = tie(pu, pg, hids[-1])

    g_stack = u_stack = sg = None
    for t in range(RING):
        if t > 0:
            if t >= 2:
                pg = tie(pg, h_stacks[t - 2][0])
            pg, pu = ring_hop(tie(pg, *g_done)), ring_hop(tie(pu, *u_done))
            if t < RING - 3:
                hid_turn()
            elif t == RING - 3:
                hid_turn(True)
        g_done = () if t == 0 else (g_stack[0],)
        u_done = () if t == 0 else (u_stack[0],)
        if t < RING - 1:
            g_stack, sg = kind_step(t, own, pg, xs, g_stack, wg, sg)
            u_stack, sg = kind_step(t, own, pu, xs, u_stack, wu, sg)
    pu = tie(pu, h_stacks[-1][0])
    u_stack, sg = kind_step(t, own, pu, xs, u_stack, wu, sg)
    slots = slot_last(t, own, pg, wg, sg)
    returned = exchange(slots)
    g_stack, _ = kind_step(t, own, tie(pg, slots), xs, g_stack)
    hid = ring_hop(tie(hids[-1], slots))
    h_stack, _ = kind_step(t, own, hid, gs, h_stacks[-1])
    grad_gate, grad_up, grad_down = (merge(own, s) for s in (g_stack, u_stack, h_stack))
    grad_input = gather_back(rt, tie(returned, grad_gate, grad_up, grad_down))
    return (grad_input, grad_gate, grad_up, grad_down)


def solution(mesh):
    placed = (
        P(("dp", "expert"), "etp"),
        P(("dp", "expert"), "etp"),
        P(("dp", "expert"), None),
        P(("dp", "expert"), None),
        P("expert", None, "etp"),
        P("expert", None, "etp"),
        P("expert", None, "etp"),
    )
    return jax.shard_map(
        per_device,
        mesh=mesh,
        in_specs=placed,
        out_specs=(
            P(("dp", "expert"), "etp"),
            P("expert", "dp", "etp"),
            P("expert", "dp", "etp"),
            P("expert", "dp", "etp"),
        ),
        check_vma=False,
    )
```

```python
import functools
import jax
import jax.numpy as jnp
from jax import lax
from jax.experimental import pallas as pl
from jax.experimental.pallas import tpu as pltpu
from jax.sharding import PartitionSpec as P

EXPERTS = 16
CAP = 66
PAD = 72
TOK = 128
RING = 8
ROWS = EXPERTS * CAP
HALF = ROWS // 2
WID = 512
FF = 1536
PART = FF // (2 * RING)
CH = 2 * PART
PACK = 2 * CH
TILE = 528
STEPS = HALF // TILE
F32 = jnp.float32
BF = jnp.bfloat16
NT = (((1,), (1,)), ((), ()))
NN = (((1,), (0,)), ((), ()))
TN = (((0,), (0,)), ((), ()))


def params(mib=20):
    return pltpu.CompilerParams(
        dimension_semantics=("arbitrary",), vmem_limit_bytes=mib * 1024 * 1024
    )


def cost(flops, nbytes):
    return pl.CostEstimate(flops=flops, bytes_accessed=nbytes, transcendentals=0)


def one_hot(first, count, rt):
    ids = lax.broadcasted_iota(jnp.int32, (count, 8, TOK), 0) + first
    match = jnp.where(rt[None] == ids, 1.0, 0.0)
    member = jnp.sum(match, axis=1)
    below = lax.broadcasted_iota(jnp.int32, (TOK, TOK), 0) < lax.broadcasted_iota(
        jnp.int32, (TOK, TOK), 1
    )
    before = lax.dot_general(
        member.astype(BF), jnp.where(below, 1.0, 0.0).astype(BF), NN, preferred_element_type=F32
    )
    place = jnp.where(member > 0.0, before, -1.0)
    slot = lax.broadcasted_iota(jnp.int32, (count, PAD, TOK), 1).astype(F32)
    return jnp.where(place[:, None, :] == slot, 1.0, 0.0), match


def slots_kernel(rt_ref, nt_ref, v_ref, o_ref):
    count = o_ref.shape[0]
    pick, match = one_hot(pl.program_id(0) * count, count, rt_ref[...])
    flat = pick.reshape(count * PAD, TOK).astype(BF)
    rows = lax.dot_general(flat, v_ref[...], NN, preferred_element_type=F32)
    rows = rows.reshape(count, PAD, WID)
    if nt_ref is not None:
        num = nt_ref[...].astype(F32)
        share = num / jnp.sum(num, axis=0, keepdims=True)
        weight = jnp.sum(match * share[None], axis=1)
        rows = rows * jnp.sum(pick * weight[:, None, :], axis=2, keepdims=True)
    o_ref[...] = rows[:, :CAP].astype(BF)


def plain_slots_kernel(rt_ref, v_ref, o_ref):
    slots_kernel(rt_ref, None, v_ref, o_ref)


def build_slots(rt, nt, values):
    count = EXPERTS
    whole = lambda x: pl.BlockSpec(x.shape, lambda i: (0, 0))
    args = [rt, values] if nt is None else [rt, nt, values]
    return pl.pallas_call(
        plain_slots_kernel if nt is None else slots_kernel,
        grid=(EXPERTS // count,),
        in_specs=[whole(x) for x in args],
        out_specs=pl.BlockSpec((count, CAP, WID), lambda i: (i, 0, 0)),
        out_shape=jax.ShapeDtypeStruct((EXPERTS, CAP, WID), BF),
        compiler_params=params(56),
        cost_estimate=cost(2 * EXPERTS * PAD * TOK * WID, 1_500_000),
        name="build_slots",
    )(*args)


def regroup_kernel(v_ref, o_ref, wide):
    for s in range(EXPERTS // 2):
        wide[CAP * s : CAP * (s + 1), :] = v_ref[s].astype(F32)
    o_ref[0] = wide[...].astype(BF)


def regroup(values):
    return pl.pallas_call(
        regroup_kernel,
        grid=(2,),
        in_specs=[pl.BlockSpec((EXPERTS // 2, CAP, WID), lambda i: (i, 0, 0))],
        out_specs=pl.BlockSpec((1, HALF, WID), lambda i: (i, 0, 0)),
        out_shape=jax.ShapeDtypeStruct((2, HALF, WID), BF),
        scratch_shapes=[pltpu.VMEM((HALF, WID), F32)],
        compiler_params=params(),
        cost_estimate=cost(1000, 2_200_000),
        name="regroup",
    )(values)


def back_kernel(rt_ref, v_ref, o_ref, acc, wide):
    count = v_ref.shape[0]
    pick, _ = one_hot(pl.program_id(0) * count, count, rt_ref[...])
    wide[...] = jnp.zeros_like(wide)
    wide[:, :CAP, :] = v_ref[...].astype(F32)
    part = lax.dot_general(
        pick.reshape(count * PAD, TOK).astype(BF),
        wide[...].reshape(count * PAD, WID).astype(BF),
        TN,
        preferred_element_type=F32,
    )

    @pl.when(pl.program_id(0) == 0)
    def _():
        acc[...] = part

    @pl.when(pl.program_id(0) > 0)
    def _():
        acc[...] += part

    @pl.when(pl.program_id(0) == pl.num_programs(0) - 1)
    def _():
        o_ref[...] = acc[...].astype(BF)


def gather_back(rt, values):
    count = EXPERTS
    return pl.pallas_call(
        back_kernel,
        grid=(EXPERTS // count,),
        in_specs=[
            pl.BlockSpec((8, TOK), lambda i: (0, 0)),
            pl.BlockSpec((count, CAP, WID), lambda i: (i, 0, 0)),
        ],
        out_specs=pl.BlockSpec((TOK, WID), lambda i: (0, 0)),
        out_shape=jax.ShapeDtypeStruct((TOK, WID), BF),
        scratch_shapes=[pltpu.VMEM((TOK, WID), F32), pltpu.VMEM((count, PAD, WID), F32)],
        compiler_params=params(),
        name="gather_back",
    )(rt, values)


def padded(w_ref):
    w = w_ref[...].reshape(CH, WID)
    zero = jnp.zeros((64, WID), BF)
    return jnp.concatenate([w, zero], axis=0), jnp.concatenate([zero, w], axis=0)


def partial_sums(rows_ref, w_ref, recv_ref):
    low, high = padded(w_ref)
    d1 = lax.dot_general(rows_ref[0], low, NT, preferred_element_type=F32)
    d2 = lax.dot_general(rows_ref[1], high, NT, preferred_element_type=F32)
    blocks = [d1[:, :128], d1[:, 128:] + d2[:, :128], d2[:, 128:]]
    if recv_ref is not None:
        blocks = [b + recv_ref[:, 128 * i : 128 * (i + 1)].astype(F32) for i, b in enumerate(blocks)]
    return blocks


def rs_kernel(first, own_ref, rows_ref, w_ref, *rest):
    recv_ref, o_ref = (None, rest[0]) if first else rest
    for i, b in enumerate(partial_sums(rows_ref, w_ref, recv_ref)):
        o_ref[:, 128 * i : 128 * (i + 1)] = b.astype(BF)


ROW_SPEC = pl.BlockSpec((2, TILE, WID), lambda i, own: (0, i, 0))
PACK_SPEC = pl.BlockSpec((TILE, PACK), lambda i, own: (i, 0))
CHUNK_SPEC = pl.BlockSpec((2, PART, WID), lambda i, own: (0, 0, 0))
PACK_BF = jax.ShapeDtypeStruct((HALF, PACK), BF)
PACK_F32 = jax.ShapeDtypeStruct((HALF, PACK), F32)


def w_spec(t):
    return pl.BlockSpec((2, PART, WID), lambda i, own: (0, own[t], 0))


def call(kernel, name, in_specs, out_specs, out_shape, flops, nbytes, scratch=(), aliases=None):
    return pl.pallas_call(
        kernel,
        grid_spec=pltpu.PrefetchScalarGridSpec(
            num_scalar_prefetch=1,
            grid=(STEPS,),
            in_specs=in_specs,
            out_specs=out_specs,
            scratch_shapes=scratch,
        ),
        out_shape=out_shape,
        input_output_aliases=aliases or {},
        compiler_params=params(),
        cost_estimate=cost(flops, nbytes),
        name=name,
    )


PROD = 2 * ROWS * CH * WID


def rs_step(t, own, rows, w, recv):
    first = recv is None
    return call(
        functools.partial(rs_kernel, first),
        "rs_step",
        [ROW_SPEC, CHUNK_SPEC if first else w_spec(t)] + ([] if first else [PACK_SPEC]),
        PACK_SPEC,
        PACK_BF,
        PROD,
        2_500_000,
    )(own, rows, w, *(() if first else (recv,)))


def hidden_kernel(own_ref, rows_ref, wg_ref, wu_ref, rg_ref, ru_ref, gp_ref, up_ref, h_ref):
    gate = partial_sums(rows_ref, wg_ref, rg_ref)
    up = partial_sums(rows_ref, wu_ref, ru_ref)
    for i in range(3):
        lanes = slice(128 * i, 128 * (i + 1))
        gp_ref[:, lanes] = gate[i]
        up_ref[:, lanes] = up[i]
        h_ref[:, lanes] = (gate[i] * jax.nn.sigmoid(gate[i]) * up[i]).astype(BF)


def hidden_step(own, rows, wg, wu, rg, ru):
    return call(
        hidden_kernel,
        "hidden_step",
        [ROW_SPEC, w_spec(0), w_spec(0), PACK_SPEC, PACK_SPEC],
        [PACK_SPEC] * 3,
        [PACK_F32, PACK_F32, PACK_BF],
        2 * PROD,
        5_000_000,
    )(own, rows, wg, wu, rg, ru)


def grads_kernel(own_ref, rows_ref, w_ref, r_ref, gp_ref, up_ref, gg_ref, gu_ref):
    grad = partial_sums(rows_ref, w_ref, r_ref)
    for i in range(3):
        lanes = slice(128 * i, 128 * (i + 1))
        gate, up = gp_ref[:, lanes], up_ref[:, lanes]
        sig = jax.nn.sigmoid(gate)
        gg_ref[:, lanes] = (grad[i] * up * sig * (1.0 + gate * (1.0 - sig))).astype(BF)
        gu_ref[:, lanes] = (grad[i] * (gate * sig)).astype(BF)


def grads_step(own, rows, w, recv, gate, up):
    return call(
        grads_kernel,
        "grads_step",
        [ROW_SPEC, w_spec(0), PACK_SPEC, PACK_SPEC, PACK_SPEC],
        [PACK_SPEC] * 2,
        [PACK_BF] * 2,
        PROD,
        5_000_000,
    )(own, rows, w, recv, gate, up)


def weight_grad(piece, rows_ref):
    a = lax.dot_general(piece[:, : CH + 64], rows_ref[0], TN, preferred_element_type=F32)
    b = lax.dot_general(piece[:, CH - 64 :], rows_ref[1], TN, preferred_element_type=F32)
    return a[:CH] + b[64:]


def grad_chunk(own_ref, piece, rows_ref, acc, keep_ref, send_ref):
    part = weight_grad(piece, rows_ref)

    @pl.when(pl.program_id(0) == 0)
    def _():
        acc[...] = part

    @pl.when(pl.program_id(0) > 0)
    def _():
        acc[...] += part

    @pl.when(pl.program_id(0) == STEPS - 1)
    def _():
        mine = own_ref[RING] == 0
        low, high = acc[:PART].astype(BF), acc[PART:].astype(BF)
        keep_ref[0] = jnp.where(mine, low, high)
        send_ref[0] = jnp.where(mine, high, low)


def slot_sums(p_ref, w_ref, sums):
    low, high = padded(w_ref)
    return [
        sums[0] + lax.dot_general(p_ref[:, : CH + 64], low, NN, preferred_element_type=F32),
        sums[1] + lax.dot_general(p_ref[:, CH - 64 :], high, NN, preferred_element_type=F32),
    ]


def kind_kernel(slots, stacked, summed, own_ref, p_ref, rows_ref, *rest):
    w_ref = rest[0] if slots else None
    sg_ref = rest[1] if slots and summed else None
    keep_ref, send_ref = rest[-3 - slots], rest[-2 - slots]
    if slots:
        out_ref = rest[-2]
        sums = [sg_ref[0], sg_ref[1]] if summed else [0.0, 0.0]
        sums = slot_sums(p_ref, w_ref, sums)
        for h in range(2):
            out_ref[h] = sums[h]
    grad_chunk(own_ref, p_ref[...], rows_ref, rest[-1], keep_ref, send_ref)


STACK = jax.ShapeDtypeStruct((RING, PART, WID), BF)
SUMS = jax.ShapeDtypeStruct((2, HALF, WID), F32)
ANY = pl.BlockSpec(memory_space=pl.ANY)


def kind_step(t, own, piece, rows, stacks, w=None, sg=None):
    slots, stacked, summed = w is not None, stacks is not None, sg is not None
    in_specs, args = [PACK_SPEC, ROW_SPEC], [piece, rows]
    if slots:
        in_specs, args = in_specs + [w_spec(t)], args + [w]
    aliases = {}
    if summed:
        aliases[len(args) + 1] = 2
        in_specs, args = in_specs + [ROW_SPEC], args + [sg]
    if stacked:
        aliases[len(args) + 1], aliases[len(args) + 2] = 0, 1
        in_specs, args = in_specs + [ANY, ANY], args + list(stacks)
    one = pl.BlockSpec((1, PART, WID), lambda i, own: (t, 0, 0))
    out = call(
        functools.partial(kind_kernel, slots, stacked, summed),
        "kind_step",
        in_specs,
        [one, one] + [ROW_SPEC] * slots,
        [STACK, STACK] + [SUMS] * slots,
        (2 if slots else 1) * PROD,
        6_000_000 if slots else 2_000_000,
        [pltpu.VMEM((CH, WID), F32)],
        aliases,
    )(own, *args)
    return out[:2], (out[2] if slots else None)


def slot_last_kernel(own_ref, p_ref, w_ref, sg_ref, o_ref, acc):
    sums = slot_sums(p_ref, w_ref, [sg_ref[0], sg_ref[1]])
    for h in range(2):
        acc[...] = sums[h]
        for s in range(EXPERTS // 2):
            o_ref[h * (EXPERTS // 2) + s] = acc[CAP * s : CAP * (s + 1), :].astype(BF)


def slot_last(t, own, piece, w, sg):
    whole = lambda shape: pl.BlockSpec(shape, lambda i, own: (0,) * len(shape))
    return pl.pallas_call(
        slot_last_kernel,
        grid_spec=pltpu.PrefetchScalarGridSpec(
            num_scalar_prefetch=1,
            grid=(1,),
            in_specs=[whole((HALF, PACK)), w_spec(t), whole((2, HALF, WID))],
            out_specs=whole((EXPERTS, CAP, WID)),
            scratch_shapes=[pltpu.VMEM((HALF, WID), F32)],
        ),
        out_shape=jax.ShapeDtypeStruct((EXPERTS, CAP, WID), BF),
        compiler_params=params(16),
        cost_estimate=cost(PROD, 4_500_000),
        name="slot_last",
    )(own, piece, w, sg)


def merge_kernel(own_ref, keep_ref, recv_ref, o_ref):
    for t in range(RING):
        place = pl.ds(pl.multiple_of(own_ref[t] * PART, PART), PART)
        total = keep_ref[t].astype(F32) + recv_ref[(RING - t) % RING].astype(F32)
        o_ref[place, :] = total.astype(BF)


def merge(own, stacks):
    keep, recv = stacks[0], lax.ppermute(stacks[1], "dp", [(0, 1), (1, 0)])
    whole = pl.BlockSpec((RING, PART, WID), lambda i, own: (0, 0, 0))
    return pl.pallas_call(
        merge_kernel,
        grid_spec=pltpu.PrefetchScalarGridSpec(
            num_scalar_prefetch=1,
            grid=(1,),
            in_specs=[whole, whole],
            out_specs=pl.BlockSpec((FF // 2, WID), lambda i, own: (0, 0)),
        ),
        out_shape=jax.ShapeDtypeStruct((FF // 2, WID), BF),
        compiler_params=params(),
        name="merge",
    )(own, keep, recv)[None]


def ring_hop(x):
    up = [(i, (i + 1) % RING) for i in range(RING)]
    down = [(RING + i, RING + (i - 1) % RING) for i in range(RING)]
    return lax.ppermute(x, ("dp", "etp"), up + down)


def tie(x, *after):
    return lax.optimization_barrier((x, *after))[0]


def exchange(x):
    return lax.all_to_all(x, "expert", split_axis=0, concat_axis=0, tiled=True)


def per_device(tokens_in, grad_output, routes, route_numer, w_gate, w_up, w_down):
    dp, z = lax.axis_index("dp"), lax.axis_index("etp")
    sign = 1 - 2 * dp
    hops = jnp.arange(RING, dtype=jnp.int32)
    own = jnp.concatenate([(z - sign * hops) % RING, dp[None]]).astype(jnp.int32)
    wg, wu, wd = (w.reshape(2, FF // 2, WID) for w in (w_gate, w_up, w_down))
    rt, nt = routes.T, route_numer.T

    x_recv = exchange(build_slots(rt, None, tokens_in))
    g_send = build_slots(rt, nt, grad_output)
    g_recv = exchange(g_send)

    wg1, wu1, wd1 = (lax.dynamic_slice_in_dim(w, own[1] * PART, PART, 1) for w in (wg, wu, wd))
    xs = regroup(tie(x_recv, g_send, wd1))
    gate, up = rs_step(1, own, xs, wg1, None), rs_step(1, own, xs, wu1, None)
    back = None
    for t in range(2, RING + 1):
        gate, up = ring_hop(gate), ring_hop(up)
        if t > 2:
            back_recv = ring_hop(back)
            gate = tie(gate, back)
        if t < RING:
            gate, up = rs_step(t, own, xs, wg, gate), rs_step(t, own, xs, wu, up)
        else:
            gate_pre, up_pre, hid = hidden_step(own, xs, wg, wu, gate, up)
        if t == 2:
            gs = regroup(tie(g_recv, gate, up))
            back = rs_step(1, own, gs, wd1, None)
        else:
            back_recv = tie(back_recv, *((gate, up) if t < RING else (hid,)))
            back = rs_step(t - 1, own, gs, wd, back_recv)
    back_recv = ring_hop(back)

    hids, h_stacks = [hid], []

    def hid_turn(last=False):
        t, piece = len(hids) - 1, hids[-1]
        if not last:
            hids.append(ring_hop(tie(piece, h_stacks[t - 3][0]) if t >= 3 else piece))
        h_stacks.append(kind_step(t, own, piece, gs, h_stacks[-1] if t else None)[0])

    hid_turn()
    hid_turn()
    pg, pu = grads_step(own, gs, wd, back_recv, gate_pre, up_pre)
    pu = tie(pu, pg, hids[-1])

    g_stack = u_stack = sg = None
    for t in range(RING):
        if t > 0:
            if t >= 2:
                pg = tie(pg, h_stacks[t - 2][0])
            pg, pu = ring_hop(tie(pg, *g_done)), ring_hop(tie(pu, *u_done))
            if t < RING - 3:
                hid_turn()
            elif t == RING - 3:
                hid_turn(True)
        g_done = () if t == 0 else (g_stack[0],)
        u_done = () if t == 0 else (u_stack[0],)
        if t < RING - 1:
            g_stack, sg = kind_step(t, own, pg, xs, g_stack, wg, sg)
            u_stack, sg = kind_step(t, own, pu, xs, u_stack, wu, sg)
    pu = tie(pu, h_stacks[-1][0])
    u_stack, sg = kind_step(t, own, pu, xs, u_stack, wu, sg)
    slots = slot_last(t, own, pg, wg, sg)
    returned = exchange(slots)
    g_stack, _ = kind_step(t, own, tie(pg, slots), xs, g_stack)
    hid = ring_hop(tie(hids[-1], slots))
    h_stack, _ = kind_step(t, own, hid, gs, h_stacks[-1])
    grad_gate, grad_up, grad_down = (merge(own, s) for s in (g_stack, u_stack, h_stack))
    grad_input = gather_back(rt, tie(returned, grad_gate, grad_up, grad_down))
    return (grad_input, grad_gate, grad_up, grad_down)


def solution(mesh):
    placed = (
        P(("dp", "expert"), "etp"),
        P(("dp", "expert"), "etp"),
        P(("dp", "expert"), None),
        P(("dp", "expert"), None),
        P("expert", None, "etp"),
        P("expert", None, "etp"),
        P("expert", None, "etp"),
    )
    return jax.shard_map(
        per_device,
        mesh=mesh,
        in_specs=placed,
        out_specs=(
            P(("dp", "expert"), "etp"),
            P("expert", "dp", "etp"),
            P("expert", "dp", "etp"),
            P("expert", "dp", "etp"),
        ),
        check_vma=False,
    )
```
